32 devices in a mesh: section: 4 (over y, x), seq: 8 (over z, core).
Axes of the slice: x: 2, y: 2, z: 4, core: 2. Of those that a mesh axis runs over, the one named last changes fastest.
Arguments:
- grad_out: bfloat16 [4, 512, 1024], P('section', 'seq'), may hold values from -6 to 6
- step_sizes: float32 [4, 16, 1024], P('section', None, 'seq'), may hold values from 0.01 to 0.1
- decay_rate: float32 [4, 16], P('section', 'seq'), may hold values from 0.001 to 1
- skip_gain: float32 [4, 16], P('section', 'seq'), may hold values from 0.5 to 1.5
- state_in: bfloat16 [4, 8, 1024, 128], P('section', None, 'seq'), may hold values from -6 to 6
- state_out: bfloat16 [4, 8, 1024, 128], P('section', None, 'seq'), may hold values from -0.5 to 0.5
- segment_ids: int32 [4, 1024], P('section'), may hold values from 0 to 15, never falling along the last dimension, each value on 1 to 512 neighbouring positions
Outputs:
- incoming: bfloat16 [4, 512, 1024], P('section', 'seq')
The draws below stay inside these ranges and needn't reach their ends.
All inputs are finite; a program needn't handle non-finite values.
Results may differ from the reference program's by a relative error of at most 0.007.
Values may be sent and summed in bfloat16 or wider, within the bound.
A program may use at most 64 MiB of HBM per device.

```python
import math
import jax
import jax.numpy as jnp
import numpy as np
from jax import lax

SEQLEN = 1024
SECTIONS = 4
HEADS = 16
HEAD_DIM = 32
STATE = 128
GROUPS = 8
SPAN = 256
DOCS = 16


def block_scale(own_key, shape, pieces, smallest, high):
    loudness, own = 1.0, jax.random.fold_in(own_key, 6)
    for dim, blocks in pieces:
        draws = jnp.exp(jax.random.uniform(jax.random.fold_in(own, dim), (blocks,), jnp.float32, smallest / len(pieces), high / len(pieces)))
        loudness = loudness * jnp.repeat(draws, shape[dim] // blocks).reshape([-1 if axis == dim else 1 for axis in range(len(shape))])
    return loudness


def profile(number_of, total, reach, skew):
    portions = [(1 << 20) // math.isqrt(rank ** skew) + 1 for rank in range(2, number_of + 1)]
    rest, holding = total - reach - (number_of - 1), [1] * (number_of - 1)
    while rest > 0:
        candidates = [i for i in range(number_of - 1) if holding[i] < reach]
        whole, remaining = sum([portions[i] for i in candidates]), rest
        for i in candidates:
            addition = min(reach - holding[i], max(1, remaining * portions[i] // whole), rest)
            holding[i] = holding[i] + addition
            rest = rest - addition
    return np.array([reach] + holding)


def uneven(rng, amount, total, limit, slope):
    if amount == 2:
        one = jax.random.randint(rng, (), max(1, total - limit), min(limit, total - 1) + 1)
        return jnp.stack([one, total - one])
    tallies = jnp.asarray(profile(amount, total, limit, slope), jnp.int32)
    twos = (amount - 1) // 2
    donor, taker = tallies[1:1 + 2 * twos:2], tallies[2:2 + 2 * twos:2]
    room = jnp.minimum(donor - 1, limit - taker)
    shifted = jax.random.randint(jax.random.fold_in(rng, 1), (twos,), 0, 1 << 20) % (room + 1)
    tallies = tallies.at[1:1 + 2 * twos:2].set(donor - shifted).at[2:2 + 2 * twos:2].set(taker + shifted)
    return tallies[jax.random.permutation(jax.random.fold_in(rng, 2), amount)]


def normal_values(own_key, extent, scale, bound, shards=(), held_as=jnp.bfloat16):
    factor_of = block_scale(own_key, extent, shards, -0.22, 0.18) if shards else 1.0
    array = jax.random.normal(own_key, extent, jnp.float32) * scale * factor_of
    return jnp.minimum(jnp.maximum(array, -bound), bound).astype(held_as)


def setup_inputs(seed: int = 0) -> dict:
    key_of = jax.random.split(jax.random.key(seed), 8)
    grad_out = normal_values(key_of[0], (SECTIONS, HEADS * HEAD_DIM, SEQLEN), 1.0, 6.0, ((0, 4), (1, 8)))
    step_sizes = jnp.clip(jnp.exp(math.log(0.1) - 2.3025851 * jax.random.uniform(key_of[1], (SECTIONS, HEADS, SEQLEN), jnp.float32) ** block_scale(key_of[1], (SECTIONS, HEADS, SEQLEN), ((0, 4), (2, 8)), -0.2, 0.2)), 0.01, 0.1)
    decay_rate = jnp.clip(jnp.exp(math.log(1.0) - 6.9077552 * jax.random.uniform(key_of[2], (SECTIONS, HEADS), jnp.float32) ** block_scale(key_of[2], (SECTIONS, HEADS), ((0, 4), (1, 8)), -0.2, 0.2)), 0.001, 1.0)
    skip_gain = jnp.clip(0.5 + 1.0 * jax.random.uniform(key_of[3], (SECTIONS, HEADS), jnp.float32) ** block_scale(key_of[3], (SECTIONS, HEADS), ((0, 4), (1, 8)), -0.2, 0.2), 0.5, 1.5)
    state_in = normal_values(key_of[4], (SECTIONS, GROUPS, SEQLEN, STATE), 1.0, 6.0, ((0, 4), (2, 8)))
    state_out = normal_values(key_of[5], (SECTIONS, GROUPS, SEQLEN, STATE), STATE ** -0.5, 0.5, ((0, 4), (2, 8)))
    segment_ids = jax.vmap(lambda own: jnp.searchsorted(jnp.cumsum(uneven(own, DOCS, SEQLEN, SEQLEN // 2, 2)), jnp.arange(SEQLEN), side="right"))(jax.random.split(key_of[6], SECTIONS)).reshape((SECTIONS, SEQLEN)).astype(jnp.int32)
    return dict(grad_out=grad_out, step_sizes=step_sizes, decay_rate=decay_rate, skip_gain=skip_gain, state_in=state_in, state_out=state_out, segment_ids=segment_ids)


def block_grad(write_block, read_block, seg_block, within_block, total_block, end_block, right_block, grad_block, step_block, skip_local):
    scores = jnp.einsum('ctn,csn->cts', read_block.astype(jnp.float32), write_block.astype(jnp.float32))
    position = jnp.arange(read_block.shape[1])
    causal = position[:, None] >= position[None, :]
    allowed = (seg_block[:, :, None] == seg_block[:, None, :]) & causal[None]
    log_gap = within_block[:, :, :, None] - within_block[:, :, None, :]
    weights = jnp.where(allowed[None], scores[None] * jnp.exp(jnp.where(allowed[None], log_gap, 0.0)), 0.0).astype(jnp.bfloat16)
    within_sum = jnp.einsum('hpct,hcts->hpcs', grad_block.astype(jnp.float32), weights.astype(jnp.float32))
    carried = jnp.einsum('chnp,csn->hpcs', right_block, write_block.astype(jnp.float32), precision=lax.Precision.HIGHEST)
    end_match = (seg_block == end_block[:, None]).astype(jnp.float32)
    carried_sum = carried * (jnp.exp(total_block[:, :, None] - within_block) * end_match[None])[:, None]
    grad_in = step_block[:, None] * (within_sum + carried_sum) + skip_local[:, None, None, None] * grad_block.astype(jnp.float32)
    return grad_in.reshape(grad_block.shape[0] * grad_block.shape[1], -1).astype(jnp.bfloat16)

def group_grad(grad_local, step_local, decay_local, skip_local, write_rows, read_rows, seg_local):
    head_count = step_local.shape[0]
    head_width = grad_local.shape[0] // head_count
    seqlen = write_rows.shape[0]
    span_count = seqlen // SPAN
    width = write_rows.shape[1]
    log_step = -decay_local[:, None] * step_local
    within = jnp.cumsum(log_step.reshape(head_count, span_count, SPAN), axis=2)
    span_total = within[:, :, -1]
    seg_span = seg_local.reshape(span_count, SPAN)
    seg_end = seg_span[:, -1]
    prev_end = jnp.concatenate([seg_end[:1], seg_end[:-1]])
    kept = (seg_span == prev_end[:, None]).astype(jnp.float32)
    read_spans = read_rows.reshape(span_count, SPAN, width)
    write_spans = write_rows.reshape(span_count, SPAN, width)
    read_scaled = (read_spans[None].astype(jnp.float32) * (jnp.exp(within) * kept[None])[..., None]).astype(jnp.bfloat16)
    grad_spans = grad_local.reshape(head_count, head_width, span_count, SPAN)
    local_state = jnp.einsum('hctn,hpct->hcnp', read_scaled.astype(jnp.float32), grad_spans.astype(jnp.float32))
    joined = seg_end == prev_end
    factor = jnp.where(joined[None, :], jnp.exp(span_total), 0.0)

    def recur(state_now, inputs):
        span_state, span_decay = inputs
        return (span_state + span_decay[:, None, None] * state_now, state_now)
    start_state = jnp.zeros((head_count, width, head_width), jnp.float32)
    _, right_state = lax.scan(recur, start_state, (jnp.transpose(local_state, (1, 0, 2, 3)), factor.T), reverse=True)
    step_spans = step_local.reshape(head_count, span_count, SPAN)
    return block_grad(write_spans, read_spans, seg_span, within, span_total, seg_end, right_state, grad_spans, step_spans, skip_local)

def reference(grad_out, step_sizes, decay_rate, skip_gain, state_in, state_out, segment_ids):
    heads_per = HEADS // GROUPS

    def section_grad(inputs):
        grad_local, step_local, decay_local, skip_local, write_all, read_all, seg_local = inputs

        def group_step(group_inputs):
            g_grad, g_step, g_decay, g_skip, g_write, g_read = group_inputs
            return group_grad(g_grad, g_step, g_decay, g_skip, g_write, g_read, seg_local)
        result = lax.map(group_step, (grad_local.reshape(GROUPS, heads_per * HEAD_DIM, SEQLEN), step_local.reshape(GROUPS, heads_per, SEQLEN), decay_local.reshape(GROUPS, heads_per), skip_local.reshape(GROUPS, heads_per), write_all, read_all))
        return result.reshape(HEADS * HEAD_DIM, SEQLEN)
    grad_in = lax.map(section_grad, (grad_out, step_sizes, decay_rate, skip_gain, state_in, state_out, segment_ids))
    return jnp.concatenate([grad_in[1:], jnp.zeros_like(grad_in[:1])], axis=0)
```

```python
import functools

import jax
import jax.numpy as jnp
from jax import lax
from jax.experimental import pallas as pl
from jax.experimental.pallas import tpu as pltpu
from jax.sharding import PartitionSpec as P

SPAN = 256
MESH = pl.DeviceIdType.MESH
F32, BF16 = jnp.float32, jnp.bfloat16


def dot_nt(a, b):
    return lax.dot_general(a, b, (((1,), (1,)), ((), ())), preferred_element_type=F32)


def dot_nn(a, b):
    return jnp.dot(a, b, preferred_element_type=F32)


def kernel(
    sections, devs,
    grad_ref, step_ref, decay_ref, skip_ref, in_ref, out_proj_ref, seg_ref,
    res_ref,
    gains_send, gains, decay, steps, write, read, grad, scaled, kept_scaled, scores, inner, local_state,
    right, right_send, result, zeros,
    grad_send, grad_recv, gain_send, gain_recv, pair_send, pair_recv, own_sem, right_send_sem, right_recv,
    res_send, res_recv, zero_sem,
):
    half = devs // 2
    spans = devs // 2
    rows, heads_dev = grad_ref.shape[1], decay_ref.shape[1]
    width = rows // heads_dev
    tok = step_ref.shape[2]
    groups = in_ref.shape[1]
    core_groups = groups // 2
    core_heads = half * heads_dev
    group_devs = devs // groups
    group_rows = group_devs * rows
    group_heads = group_devs * heads_dev

    section = lax.axis_index("section")
    me = lax.axis_index("seq")
    span = me // 2
    core = me % 2
    sibling = 2 * span + 1 - core
    owner_core = me // half
    slot = me - owner_core * half
    base = pl.multiple_of(span * SPAN, SPAN)
    last_section = sections - 1
    last_span = spans - 1
    barrier = pltpu.get_barrier_semaphore()

    def signal(sec, seq):
        pl.semaphore_signal(barrier, inc=1, device_id=(sec, seq), device_id_type=MESH)

    def landed(region, sem):
        pltpu.make_async_copy(region, region, sem).wait()

    @pl.when(section > 0)
    def _():
        for j in range(half):
            source = core * half + j

            @pl.when(source != me)
            def _():
                signal(section, source)

        signal(section, sibling)

        @pl.when(span < last_span)
        def _():
            signal(section, me + 2)

    @pl.when(section < last_section)
    def _():
        for z in range(spans):
            signal(section + 1, 2 * z + owner_core)

    own_tok = pl.ds(pl.multiple_of(core * tok, tok), tok)
    sib_tok = pl.ds(pl.multiple_of((1 - core) * tok, tok), tok)
    own_groups = pl.ds(core * core_groups, core_groups)
    sib_groups = pl.ds((1 - core) * core_groups, core_groups)
    own_heads = pl.ds(pl.multiple_of(core * core_heads, core_heads), core_heads)
    sib_heads = pl.ds(pl.multiple_of((1 - core) * core_heads, core_heads), core_heads)

    zero_copy = pltpu.make_async_copy(zeros, res_ref.at[0], zero_sem)

    @pl.when(section == last_section)
    def _():
        zeros[...] = jnp.zeros_like(zeros)
        zero_copy.start()

    @pl.when(section > 0)
    def _():
        own = [
            pltpu.make_async_copy(step_ref.at[0, own_heads, :], steps.at[:, own_tok], own_sem.at[0]),
            pltpu.make_async_copy(in_ref.at[0, own_groups], write.at[:, own_tok, :], own_sem.at[1]),
            pltpu.make_async_copy(out_proj_ref.at[0, own_groups], read.at[:, own_tok, :], own_sem.at[2]),
        ]
        for copy in own:
            copy.start()
        for i in range(heads_dev):
            gains_send[i : i + 1, :] = jnp.full((1, SPAN), decay_ref[0, i], F32)
            gains_send[heads_dev + i : heads_dev + i + 1, :] = jnp.full((1, SPAN), skip_ref[0, i], F32)

        to_self = (core == owner_core).astype(jnp.int32)
        after_first = (span > 0).astype(jnp.int32)
        pl.semaphore_wait(barrier, half - to_self + 1 + after_first + half)

        sends = []
        grad_slot = pl.ds(pl.multiple_of(slot * rows, rows), rows)
        for z in reversed(range(spans)):
            target = 2 * z + owner_core
            there = target != me
            piece = grad_ref.at[0, :, pl.ds(z * SPAN, SPAN)]
            grad_copy = pltpu.make_async_remote_copy(
                src_ref=piece, dst_ref=grad.at[grad_slot, :], send_sem=grad_send.at[z], recv_sem=grad_recv.at[slot],
                device_id=(section, target), device_id_type=MESH,
            )
            gain_copy = pltpu.make_async_remote_copy(
                src_ref=gains_send, dst_ref=gains.at[slot], send_sem=gain_send.at[z], recv_sem=gain_recv.at[slot],
                device_id=(section, target), device_id_type=MESH,
            )

            @pl.when(there)
            def _():
                gain_copy.start()
                grad_copy.start()

            @pl.when(jnp.logical_not(there))
            def _():
                pltpu.make_async_copy(gains_send, gains.at[slot], gain_recv.at[slot]).start()
                pltpu.make_async_copy(piece, grad.at[grad_slot, :], grad_recv.at[slot]).start()

            sends.append((there, grad_copy, gain_copy))

        pairs = []
        for number, (src, dst) in enumerate((
            (step_ref.at[0, sib_heads, :], steps.at[:, own_tok]),
            (in_ref.at[0, sib_groups], write.at[:, own_tok, :]),
            (out_proj_ref.at[0, sib_groups], read.at[:, own_tok, :]),
        )):
            copy = pltpu.make_async_remote_copy(
                src_ref=src, dst_ref=dst, send_sem=pair_send.at[number], recv_sem=pair_recv.at[number],
                device_id=(section, sibling), device_id_type=MESH,
            )
            copy.start()
            pairs.append(copy)

        seg = seg_ref[0:1, pl.ds(base, SPAN)].astype(F32)
        before = pl.multiple_of(jnp.maximum(base - 128, 0), 128)
        prev_end = seg_ref[0:1, pl.ds(before, 128)].astype(F32)[:, 127:128]
        seg_end = seg[:, SPAN - 1 : SPAN]
        kept = (seg == prev_end).astype(F32)
        end_match = (seg == seg_end).astype(F32)
        joined = (seg_end == prev_end).astype(F32)
        seg_rows = jnp.broadcast_to(seg, (SPAN, SPAN))
        t_index = lax.broadcasted_iota(jnp.int32, (SPAN, SPAN), 0)
        s_index = lax.broadcasted_iota(jnp.int32, (SPAN, SPAN), 1)
        allowed = (t_index >= s_index) & (seg_rows == seg_rows.T)
        summing = (t_index <= s_index).astype(F32)

        own[0].wait()
        landed(steps.at[:, sib_tok], pair_recv.at[0])
        step_rows = steps[...]
        running = jnp.dot(step_rows, summing, precision=lax.Precision.HIGHEST, preferred_element_type=F32)

        own[1].wait()
        own[2].wait()
        landed(write.at[:, sib_tok, :], pair_recv.at[1])
        landed(read.at[:, sib_tok, :], pair_recv.at[2])
        for g in range(core_groups):
            scores[g] = jnp.where(allowed, dot_nt(read[g], write[g]), 0.0).astype(BF16)

        for j in range(half):
            landed(gains.at[j], gain_recv.at[j])
            decay[j * heads_dev : (j + 1) * heads_dev, :] = gains[j, 0:heads_dev, :]
        within = -decay[...] * running
        grow = jnp.exp(within)
        shrink = step_rows * jnp.exp(-within)
        total = grow[:, SPAN - 1 : SPAN]
        factor = total * joined

        right_copies = []
        for g in range(core_groups):
            part = pl.ds(g * group_rows, group_rows)
            right_copies.append(pltpu.make_async_remote_copy(
                src_ref=right_send.at[part, :], dst_ref=right.at[part, :],
                send_sem=right_send_sem.at[g], recv_sem=right_recv.at[g],
                device_id=(section, me - 2), device_id_type=MESH,
            ))

        for g in range(core_groups):
            for j in range(g * group_devs, (g + 1) * group_devs):
                landed(grad.at[pl.ds(j * rows, rows), :], grad_recv.at[j])
                for i in range(heads_dev):
                    head = j * heads_dev + i
                    part = pl.ds(head * width, width)
                    grown = grad[part, :].astype(F32) * grow[head : head + 1, :]
                    scaled[part, :] = grown.astype(BF16)
                    kept_scaled[part, :] = (grown * kept).astype(BF16)
            part = pl.ds(g * group_rows, group_rows)
            local_state[part, :] = dot_nn(kept_scaled[part, :], read[g])

            @pl.when(span == last_span)
            def _():
                right[part, :] = jnp.zeros((group_rows, right.shape[1]), BF16)
                if spans > 1:
                    right_send[part, :] = local_state[part, :].astype(BF16)
                    right_copies[g].start()

        for g in range(core_groups):
            part = pl.ds(g * group_rows, group_rows)
            inner[part, :] = dot_nn(scaled[part, :], scores[g])

        for g in range(core_groups):
            part = pl.ds(g * group_rows, group_rows)

            @pl.when(span < last_span)
            def _():
                landed(right.at[part, :], right_recv.at[g])

            @pl.when((span < last_span) & (span > 0))
            def _():
                for h in range(g * group_heads, (g + 1) * group_heads):
                    piece = pl.ds(h * width, width)
                    right_send[piece, :] = (
                        local_state[piece, :] + factor[h : h + 1, :] * right[piece, :].astype(F32)
                    ).astype(BF16)
                right_copies[g].start()

        res_copies = []
        for g in range(core_groups):
            part = pl.ds(g * group_rows, group_rows)
            carried = dot_nt(right[part, :], write[g])
            for j in range(g * group_devs, (g + 1) * group_devs):
                for i in range(heads_dev):
                    head = j * heads_dev + i
                    piece = pl.ds(head * width, width)
                    first = (head - g * group_heads) * width
                    reach = end_match * total[head : head + 1, :]
                    result[piece, :] = (
                        shrink[head : head + 1, :] * (inner[piece, :] + reach * carried[first : first + width, :])
                        + gains[j, heads_dev + i : heads_dev + i + 1, :] * grad[piece, :].astype(F32)
                    ).astype(BF16)
                copy = pltpu.make_async_remote_copy(
                    src_ref=result.at[pl.ds(j * rows, rows), :], dst_ref=res_ref.at[0, :, pl.ds(base, SPAN)],
                    send_sem=res_send.at[j], recv_sem=res_recv.at[span],
                    device_id=(section - 1, core * half + j), device_id_type=MESH,
                )
                copy.start()
                res_copies.append(copy)

        for there, grad_copy, gain_copy in sends:
            @pl.when(there)
            def _():
                grad_copy.wait_send()
                gain_copy.wait_send()
        for copy in pairs:
            copy.wait_send()

        @pl.when(span > 0)
        def _():
            for copy in right_copies:
                copy.wait_send()

        for copy in res_copies:
            copy.wait_send()

    @pl.when(section < last_section)
    def _():
        for z in range(spans):
            landed(res_ref.at[0, :, pl.ds(z * SPAN, SPAN)], res_recv.at[z])

    @pl.when(section == last_section)
    def _():
        zero_copy.wait()


def solution(mesh):
    sections, devs = mesh.shape["section"], mesh.shape["seq"]
    placed = (
        P("section", "seq", None),
        P("section", None, "seq"),
        P("section", "seq"),
        P("section", "seq"),
        P("section", None, "seq", None),
        P("section", None, "seq", None),
        P("section", None),
    )

    def local(grad_out, step_sizes, decay_rate, skip_gain, state_in, state_out, segment_ids):
        rows, seqlen = grad_out.shape[1:]
        heads_dev = decay_rate.shape[1]
        groups, _, state = state_in.shape[1:]
        half = devs // 2
        all_rows = half * rows
        core_heads = half * heads_dev
        core_groups = groups // 2
        gain_rows = -(-2 * heads_dev // 8) * 8
        dma = pltpu.SemaphoreType.DMA
        anywhere = pl.BlockSpec(memory_space=pl.ANY)
        scalars = pl.BlockSpec(memory_space=pltpu.SMEM)
        return pl.pallas_call(
            functools.partial(kernel, sections, devs),
            out_shape=jax.ShapeDtypeStruct(grad_out.shape, BF16),
            in_specs=[anywhere, anywhere, scalars, scalars, anywhere, anywhere, pl.BlockSpec(memory_space=pltpu.VMEM)],
            out_specs=anywhere,
            scratch_shapes=[
                pltpu.VMEM((gain_rows, SPAN), F32),
                pltpu.VMEM((half, gain_rows, SPAN), F32),
                pltpu.VMEM((core_heads, SPAN), F32),
                pltpu.VMEM((core_heads, SPAN), F32),
                pltpu.VMEM((core_groups, SPAN, state), BF16),
                pltpu.VMEM((core_groups, SPAN, state), BF16),
                pltpu.VMEM((all_rows, SPAN), BF16),
                pltpu.VMEM((all_rows, SPAN), BF16),
                pltpu.VMEM((all_rows, SPAN), BF16),
                pltpu.VMEM((core_groups, SPAN, SPAN), BF16),
                pltpu.VMEM((all_rows, SPAN), F32),
                pltpu.VMEM((all_rows, state), F32),
                pltpu.VMEM((all_rows, state), BF16),
                pltpu.VMEM((all_rows, state), BF16),
                pltpu.VMEM((all_rows, SPAN), BF16),
                pltpu.VMEM((rows, seqlen), BF16),
                dma((half,)), dma((half,)), dma((half,)), dma((half,)),
                dma((3,)), dma((3,)), dma((3,)),
                dma((core_groups,)), dma((core_groups,)),
                dma((half,)), dma((half,)), dma,
            ],
            compiler_params=pltpu.CompilerParams(
                collective_id=0, has_side_effects=True, vmem_limit_bytes=48 * 1024 * 1024
            ),
        )(grad_out, step_sizes, decay_rate, skip_gain, state_in, state_out, segment_ids)

    return jax.shard_map(
        local, mesh=mesh, in_specs=placed, out_specs=P("section", "seq", None), check_vma=False
    )
```

```python
import functools

import jax
import jax.numpy as jnp
from jax import lax
from jax.experimental import pallas as pl
from jax.experimental.pallas import tpu as pltpu
from jax.sharding import PartitionSpec as P

SPAN = 256
MESH = pl.DeviceIdType.MESH
F32, BF16 = jnp.float32, jnp.bfloat16


def dot_nt(a, b):
    return lax.dot_general(a, b, (((1,), (1,)), ((), ())), preferred_element_type=F32)


def dot_nn(a, b):
    return jnp.dot(a, b, preferred_element_type=F32)


def kernel(
    sections, devs,
    grad_ref, step_ref, decay_hbm, skip_hbm, in_ref, out_proj_ref, seg_hbm,
    res_ref,
    decay_ref, skip_ref, seg_ref, gains_send, gains, decay, all_steps, steps, write, read, grad, scaled, kept_scaled, scores, inner, local_state,
    right, right_send, result, zeros,
    grad_send, grad_recv, gain_send, gain_recv, pair_send, pair_recv, own_sem, right_send_sem, right_recv,
    res_send, res_recv, zero_sem, small_sem,
):
    half = devs // 2
    spans = devs // 2
    rows, heads_dev = grad_ref.shape[1], decay_hbm.shape[1]
    width = rows // heads_dev
    tok = step_ref.shape[2]
    core_groups = in_ref.shape[1]
    groups = 2 * core_groups
    core_heads = half * heads_dev
    group_devs = devs // groups
    group_rows = group_devs * rows
    group_heads = group_devs * heads_dev

    section = lax.axis_index("section")
    me = lax.axis_index("seq")
    span = me // 2
    core = me % 2
    sibling = 2 * span + 1 - core
    own_group = me // group_devs
    owner_core = own_group % 2
    slot = own_group // 2 * group_devs + me % group_devs
    base = pl.multiple_of(span * SPAN, SPAN)
    last_section = sections - 1
    last_span = spans - 1
    barrier = pltpu.get_barrier_semaphore()

    def signal(sec, seq):
        pl.semaphore_signal(barrier, inc=1, device_id=(sec, seq), device_id_type=MESH)

    def device_of(j):
        return (2 * (j // group_devs) + core) * group_devs + j % group_devs

    def landed(region, sem):
        pltpu.make_async_copy(region, region, sem).wait()

    @pl.when(section > 0)
    def _():
        for j in range(half):
            source = device_of(j)

            @pl.when(source != me)
            def _():
                signal(section, source)

        signal(section, sibling)

        @pl.when(span < last_span)
        def _():
            signal(section, me + 2)

    @pl.when(section < last_section)
    def _():
        for z in range(spans):
            signal(section + 1, 2 * z + owner_core)

    own_tok = pl.ds(pl.multiple_of(core * tok, tok), tok)
    sib_tok = pl.ds(pl.multiple_of((1 - core) * tok, tok), tok)
    zero_copy = pltpu.make_async_copy(zeros, res_ref.at[0], zero_sem)

    @pl.when(section == last_section)
    def _():
        zeros[...] = jnp.zeros_like(zeros)
        zero_copy.start()

    @pl.when(section > 0)
    def _():
        small = [
            pltpu.make_async_copy(decay_hbm, decay_ref, small_sem.at[0]),
            pltpu.make_async_copy(skip_hbm, skip_ref, small_sem.at[1]),
            pltpu.make_async_copy(seg_hbm, seg_ref, small_sem.at[2]),
        ]
        own = [
            pltpu.make_async_copy(step_ref.at[0], all_steps.at[:, own_tok], own_sem.at[0]),
            pltpu.make_async_copy(in_ref.at[0, :, core], write.at[:, own_tok, :], own_sem.at[1]),
            pltpu.make_async_copy(out_proj_ref.at[0, :, core], read.at[:, own_tok, :], own_sem.at[2]),
        ]
        for copy in small + own:
            copy.start()
        for copy in small:
            copy.wait()
        for i in range(heads_dev):
            gains_send[i : i + 1, :] = jnp.full((1, SPAN), decay_ref[0, i], F32)
            gains_send[heads_dev + i : heads_dev + i + 1, :] = jnp.full((1, SPAN), skip_ref[0, i], F32)

        to_self = (core == owner_core).astype(jnp.int32)
        after_first = (span > 0).astype(jnp.int32)
        pl.semaphore_wait(barrier, half - to_self + 1 + after_first + half)

        sends = []
        grad_slot = pl.ds(pl.multiple_of(slot * rows, rows), rows)
        for z in reversed(range(spans)):
            target = 2 * z + owner_core
            there = target != me
            piece = grad_ref.at[0, :, pl.ds(z * SPAN, SPAN)]
            grad_copy = pltpu.make_async_remote_copy(
                src_ref=piece, dst_ref=grad.at[grad_slot, :], send_sem=grad_send.at[z], recv_sem=grad_recv.at[slot],
                device_id=(section, target), device_id_type=MESH,
            )
            gain_copy = pltpu.make_async_remote_copy(
                src_ref=gains_send, dst_ref=gains.at[slot], send_sem=gain_send.at[z], recv_sem=gain_recv.at[slot],
                device_id=(section, target), device_id_type=MESH,
            )

            @pl.when(there)
            def _():
                gain_copy.start()
                grad_copy.start()

            @pl.when(jnp.logical_not(there))
            def _():
                pltpu.make_async_copy(gains_send, gains.at[slot], gain_recv.at[slot]).start()
                pltpu.make_async_copy(piece, grad.at[grad_slot, :], grad_recv.at[slot]).start()

            sends.append((there, grad_copy, gain_copy))

        pairs = []
        for number, (src, dst) in enumerate((
            (step_ref.at[0], all_steps.at[:, own_tok]),
            (in_ref.at[0, :, 1 - core], write.at[:, own_tok, :]),
            (out_proj_ref.at[0, :, 1 - core], read.at[:, own_tok, :]),
        )):
            copy = pltpu.make_async_remote_copy(
                src_ref=src, dst_ref=dst, send_sem=pair_send.at[number], recv_sem=pair_recv.at[number],
                device_id=(section, sibling), device_id_type=MESH,
            )
            copy.start()
            pairs.append(copy)

        seg = seg_ref[0:1, pl.ds(base, SPAN)].astype(F32)
        before = pl.multiple_of(jnp.maximum(base - 128, 0), 128)
        prev_end = seg_ref[0:1, pl.ds(before, 128)].astype(F32)[:, 127:128]
        seg_end = seg[:, SPAN - 1 : SPAN]
        kept = (seg == prev_end).astype(F32)
        end_match = (seg == seg_end).astype(F32)
        joined = (seg_end == prev_end).astype(F32)
        seg_rows = jnp.broadcast_to(seg, (SPAN, SPAN))
        t_index = lax.broadcasted_iota(jnp.int32, (SPAN, SPAN), 0)
        s_index = lax.broadcasted_iota(jnp.int32, (SPAN, SPAN), 1)
        allowed = (t_index >= s_index) & (seg_rows == seg_rows.T)
        summing = (t_index <= s_index).astype(F32)

        own[0].wait()
        landed(all_steps.at[:, sib_tok], pair_recv.at[0])
        for g in range(core_groups):
            even = 2 * g * group_heads
            odd = even + group_heads
            steps[g * group_heads : (g + 1) * group_heads, :] = jnp.where(
                core == 0, all_steps[even : even + group_heads, :], all_steps[odd : odd + group_heads, :]
            )
        step_rows = steps[...]
        running = jnp.dot(step_rows, summing, precision=lax.Precision.HIGHEST, preferred_element_type=F32)

        own[1].wait()
        own[2].wait()
        landed(write.at[:, sib_tok, :], pair_recv.at[1])
        landed(read.at[:, sib_tok, :], pair_recv.at[2])
        for g in range(core_groups):
            scores[g] = jnp.where(allowed, dot_nt(read[g], write[g]), 0.0).astype(BF16)

        for j in range(half):
            landed(gains.at[j], gain_recv.at[j])
            decay[j * heads_dev : (j + 1) * heads_dev, :] = gains[j, 0:heads_dev, :]
        within = -decay[...] * running
        grow = jnp.exp(within)
        shrink = step_rows * jnp.exp(-within)
        total = grow[:, SPAN - 1 : SPAN]
        factor = total * joined

        right_copies = []
        for g in range(core_groups):
            part = pl.ds(g * group_rows, group_rows)
            right_copies.append(pltpu.make_async_remote_copy(
                src_ref=right_send.at[part, :], dst_ref=right.at[part, :],
                send_sem=right_send_sem.at[g], recv_sem=right_recv.at[g],
                device_id=(section, me - 2), device_id_type=MESH,
            ))

        for g in reversed(range(core_groups)):
            for j in range(g * group_devs, (g + 1) * group_devs):
                landed(grad.at[pl.ds(j * rows, rows), :], grad_recv.at[j])
                for i in range(heads_dev):
                    head = j * heads_dev + i
                    part = pl.ds(head * width, width)
                    grown = grad[part, :].astype(F32) * grow[head : head + 1, :]
                    scaled[part, :] = grown.astype(BF16)
                    kept_scaled[part, :] = (grown * kept).astype(BF16)
            part = pl.ds(g * group_rows, group_rows)
            local_state[part, :] = dot_nn(kept_scaled[part, :], read[g])

            @pl.when(span == last_span)
            def _():
                right[part, :] = jnp.zeros((group_rows, right.shape[1]), BF16)
                if spans > 1:
                    right_send[part, :] = local_state[part, :].astype(BF16)
                    right_copies[g].start()

        for g in range(core_groups):
            part = pl.ds(g * group_rows, group_rows)
            inner[part, :] = dot_nn(scaled[part, :], scores[g])

        for g in reversed(range(core_groups)):
            part = pl.ds(g * group_rows, group_rows)

            @pl.when(span < last_span)
            def _():
                landed(right.at[part, :], right_recv.at[g])

            @pl.when((span < last_span) & (span > 0))
            def _():
                for h in range(g * group_heads, (g + 1) * group_heads):
                    piece = pl.ds(h * width, width)
                    right_send[piece, :] = (
                        local_state[piece, :] + factor[h : h + 1, :] * right[piece, :].astype(F32)
                    ).astype(BF16)
                right_copies[g].start()

        res_copies = []
        for g in reversed(range(core_groups)):
            part = pl.ds(g * group_rows, group_rows)
            carried = dot_nt(right[part, :], write[g])
            for j in range(g * group_devs, (g + 1) * group_devs):
                for i in range(heads_dev):
                    head = j * heads_dev + i
                    piece = pl.ds(head * width, width)
                    first = (head - g * group_heads) * width
                    reach = end_match * total[head : head + 1, :]
                    result[piece, :] = (
                        shrink[head : head + 1, :] * (inner[piece, :] + reach * carried[first : first + width, :])
                        + gains[j, heads_dev + i : heads_dev + i + 1, :] * grad[piece, :].astype(F32)
                    ).astype(BF16)
                copy = pltpu.make_async_remote_copy(
                    src_ref=result.at[pl.ds(j * rows, rows), :], dst_ref=res_ref.at[0, :, pl.ds(base, SPAN)],
                    send_sem=res_send.at[j], recv_sem=res_recv.at[span],
                    device_id=(section - 1, device_of(j)), device_id_type=MESH,
                )
                copy.start()
                res_copies.append(copy)

        for there, grad_copy, gain_copy in sends:
            @pl.when(there)
            def _():
                grad_copy.wait_send()
                gain_copy.wait_send()
        for copy in pairs:
            copy.wait_send()

        @pl.when(span > 0)
        def _():
            for copy in right_copies:
                copy.wait_send()

        for copy in res_copies:
            copy.wait_send()

    @pl.when(section < last_section)
    def _():
        for z in range(spans):
            landed(res_ref.at[0, :, pl.ds(z * SPAN, SPAN)], res_recv.at[z])

    @pl.when(section == last_section)
    def _():
        zero_copy.wait()


def solution(mesh):
    sections, devs = mesh.shape["section"], mesh.shape["seq"]
    placed = (
        P("section", "seq", None),
        P("section", None, "seq"),
        P("section", "seq"),
        P("section", "seq"),
        P("section", None, "seq", None),
        P("section", None, "seq", None),
        P("section", None),
    )

    def local(grad_out, step_sizes, decay_rate, skip_gain, state_in, state_out, segment_ids):
        rows, seqlen = grad_out.shape[1:]
        heads_dev = decay_rate.shape[1]
        groups, tok, state = state_in.shape[1:]
        half = devs // 2
        all_rows = half * rows
        core_heads = half * heads_dev
        core_groups = groups // 2
        gain_rows = -(-2 * heads_dev // 8) * 8
        dma = pltpu.SemaphoreType.DMA
        anywhere = pl.BlockSpec(memory_space=pl.ANY)
        by_core = (1, core_groups, 2, tok, state)
        return pl.pallas_call(
            functools.partial(kernel, sections, devs),
            out_shape=jax.ShapeDtypeStruct(grad_out.shape, BF16),
            in_specs=[anywhere] * 7,
            out_specs=anywhere,
            scratch_shapes=[
                pltpu.SMEM(decay_rate.shape, F32),
                pltpu.SMEM(skip_gain.shape, F32),
                pltpu.VMEM(segment_ids.shape, jnp.int32),
                pltpu.VMEM((gain_rows, SPAN), F32),
                pltpu.VMEM((half, gain_rows, SPAN), F32),
                pltpu.VMEM((core_heads, SPAN), F32),
                pltpu.VMEM((2 * core_heads, SPAN), F32),
                pltpu.VMEM((core_heads, SPAN), F32),
                pltpu.VMEM((core_groups, SPAN, state), BF16),
                pltpu.VMEM((core_groups, SPAN, state), BF16),
                pltpu.VMEM((all_rows, SPAN), BF16),
                pltpu.VMEM((all_rows, SPAN), BF16),
                pltpu.VMEM((all_rows, SPAN), BF16),
                pltpu.VMEM((core_groups, SPAN, SPAN), BF16),
                pltpu.VMEM((all_rows, SPAN), F32),
                pltpu.VMEM((all_rows, state), F32),
                pltpu.VMEM((all_rows, state), BF16),
                pltpu.VMEM((all_rows, state), BF16),
                pltpu.VMEM((all_rows, SPAN), BF16),
                pltpu.VMEM((rows, seqlen), BF16),
                dma((half,)), dma((half,)), dma((half,)), dma((half,)),
                dma((3,)), dma((3,)), dma((3,)),
                dma((core_groups,)), dma((core_groups,)),
                dma((half,)), dma((half,)), dma, dma((3,)),
            ],
            compiler_params=pltpu.CompilerParams(
                collective_id=0, has_side_effects=True, vmem_limit_bytes=63 * 1024 * 1024
            ),
        )(
            grad_out, step_sizes, decay_rate, skip_gain,
            state_in.reshape(by_core), state_out.reshape(by_core), segment_ids,
        )

    return jax.shard_map(
        local, mesh=mesh, in_specs=placed, out_specs=P("section", "seq", None), check_vma=False
    )
```

```python
import functools

import jax
import jax.numpy as jnp
from jax import lax
from jax.experimental import pallas as pl
from jax.experimental.pallas import tpu as pltpu
from jax.sharding import PartitionSpec as P

SPAN = 256
LANES = 128
MIB = 1024 * 1024
MESH = pl.DeviceIdType.MESH
F32, BF16 = jnp.float32, jnp.bfloat16


def dot_nt(a, b):
    return lax.dot_general(a, b, (((1,), (1,)), ((), ())), preferred_element_type=F32)


def dot_nn(a, b):
    return jnp.dot(a, b, preferred_element_type=F32)


def kernel(
    sections, devs,
    grad_ref, step_ref, decay_hbm, skip_hbm, in_ref, out_proj_ref, seg_hbm,
    res_ref,
    decay_ref, skip_ref, seg_ref, gains_send, gains, decay, all_steps, steps, write, read, grad, scaled, kept_scaled, scores, inner, local_state,
    right, right_send, above, ahead, factor_send, above_factor, result, zeros,
    grad_send, grad_recv, gain_send, gain_recv, pair_send, pair_recv, own_sem, right_send_sem, right_recv,
    above_send, above_recv, ahead_send, ahead_recv, factor_sem,
    res_send, res_recv, zero_sem, small_sem,
):
    half = devs // 2
    spans = devs // 2
    rows, heads_dev = grad_ref.shape[1], decay_hbm.shape[1]
    width = rows // heads_dev
    tok = step_ref.shape[2]
    core_groups = in_ref.shape[1]
    groups = 2 * core_groups
    core_heads = half * heads_dev
    group_devs = devs // groups
    group_rows = group_devs * rows
    group_heads = group_devs * heads_dev

    section = lax.axis_index("section")
    me = lax.axis_index("seq")
    span = me // 2
    core = me % 2
    sibling = 2 * span + 1 - core
    own_group = me // group_devs
    owner_core = own_group % 2
    slot = own_group // 2 * group_devs + me % group_devs
    base = pl.multiple_of(span * SPAN, SPAN)
    last_section = sections - 1
    last_span = spans - 1
    leads = (last_span - span) % 2 == 0
    follows = jnp.logical_not(leads)
    barrier = pltpu.get_barrier_semaphore()

    def signal(sec, seq):
        pl.semaphore_signal(barrier, inc=1, device_id=(sec, seq), device_id_type=MESH)

    def device_of(j):
        return (2 * (j // group_devs) + core) * group_devs + j % group_devs

    def landed(region, sem):
        pltpu.make_async_copy(region, region, sem).wait()

    @pl.when(section > 0)
    def _():
        for j in range(half):
            source = device_of(j)

            @pl.when(source != me)
            def _():
                signal(section, source)

        signal(section, sibling)

        @pl.when(span < last_span)
        def _():
            signal(section, me + 2)

        @pl.when(leads & (span < last_span))
        def _():
            signal(section, me + 4)

    @pl.when(section < last_section)
    def _():
        for z in range(spans):
            signal(section + 1, 2 * z + owner_core)

    own_tok = pl.ds(pl.multiple_of(core * tok, tok), tok)
    sib_tok = pl.ds(pl.multiple_of((1 - core) * tok, tok), tok)
    zero_copy = pltpu.make_async_copy(zeros, res_ref.at[0], zero_sem)

    @pl.when(section == last_section)
    def _():
        zeros[...] = jnp.zeros_like(zeros)
        zero_copy.start()

    @pl.when(section > 0)
    def _():
        small = [
            pltpu.make_async_copy(decay_hbm, decay_ref, small_sem.at[0]),
            pltpu.make_async_copy(skip_hbm, skip_ref, small_sem.at[1]),
            pltpu.make_async_copy(seg_hbm, seg_ref, small_sem.at[2]),
        ]
        own = [
            pltpu.make_async_copy(step_ref.at[0], all_steps.at[:, own_tok], own_sem.at[0]),
            pltpu.make_async_copy(in_ref.at[0, :, core], write.at[:, own_tok, :], own_sem.at[1]),
            pltpu.make_async_copy(out_proj_ref.at[0, :, core], read.at[:, own_tok, :], own_sem.at[2]),
        ]
        for copy in small + own:
            copy.start()
        for copy in small:
            copy.wait()
        for i in range(heads_dev):
            gains_send[i : i + 1, :] = jnp.full((1, LANES), decay_ref[0, i], F32)
            gains_send[heads_dev + i : heads_dev + i + 1, :] = jnp.full((1, LANES), skip_ref[0, i], F32)

        to_self = (core == owner_core).astype(jnp.int32)
        after_first = (span > 0).astype(jnp.int32)
        hands_two = (leads & (span > 1)).astype(jnp.int32)
        pl.semaphore_wait(barrier, half - to_self + 1 + after_first + hands_two + half)

        sends = []
        grad_slot = pl.ds(pl.multiple_of(slot * rows, rows), rows)
        for z in reversed(range(spans)):
            target = 2 * z + owner_core
            there = target != me
            piece = grad_ref.at[0, :, pl.ds(z * SPAN, SPAN)]
            grad_copy = pltpu.make_async_remote_copy(
                src_ref=piece, dst_ref=grad.at[grad_slot, :], send_sem=grad_send.at[z], recv_sem=grad_recv.at[slot],
                device_id=(section, target), device_id_type=MESH,
            )
            gain_copy = pltpu.make_async_remote_copy(
                src_ref=gains_send, dst_ref=gains.at[slot], send_sem=gain_send.at[z], recv_sem=gain_recv.at[slot],
                device_id=(section, target), device_id_type=MESH,
            )

            @pl.when(there)
            def _():
                gain_copy.start()
                grad_copy.start()

            @pl.when(jnp.logical_not(there))
            def _():
                pltpu.make_async_copy(gains_send, gains.at[slot], gain_recv.at[slot]).start()
                pltpu.make_async_copy(piece, grad.at[grad_slot, :], grad_recv.at[slot]).start()

            sends.append((there, grad_copy, gain_copy))

        pairs = []
        for number, (src, dst) in enumerate((
            (step_ref.at[0], all_steps.at[:, own_tok]),
            (in_ref.at[0, :, 1 - core], write.at[:, own_tok, :]),
            (out_proj_ref.at[0, :, 1 - core], read.at[:, own_tok, :]),
        )):
            copy = pltpu.make_async_remote_copy(
                src_ref=src, dst_ref=dst, send_sem=pair_send.at[number], recv_sem=pair_recv.at[number],
                device_id=(section, sibling), device_id_type=MESH,
            )
            copy.start()
            pairs.append(copy)

        seg = seg_ref[0:1, pl.ds(base, SPAN)].astype(F32)
        before = pl.multiple_of(jnp.maximum(base - 128, 0), 128)
        prev_end = seg_ref[0:1, pl.ds(before, 128)].astype(F32)[:, 127:128]
        seg_end = seg[:, SPAN - 1 : SPAN]
        kept = (seg == prev_end).astype(F32)
        end_match = (seg == seg_end).astype(F32)
        joined = (seg_end == prev_end).astype(F32)
        seg_rows = jnp.broadcast_to(seg, (SPAN, SPAN))
        t_index = lax.broadcasted_iota(jnp.int32, (SPAN, SPAN), 0)
        s_index = lax.broadcasted_iota(jnp.int32, (SPAN, SPAN), 1)
        allowed = (t_index >= s_index) & (seg_rows == seg_rows.T)
        summing = (t_index <= s_index).astype(F32)

        own[0].wait()
        landed(all_steps.at[:, sib_tok], pair_recv.at[0])
        for g in range(core_groups):
            even = 2 * g * group_heads
            odd = even + group_heads
            steps[g * group_heads : (g + 1) * group_heads, :] = jnp.where(
                core == 0, all_steps[even : even + group_heads, :], all_steps[odd : odd + group_heads, :]
            )
        step_rows = steps[...]
        running = jnp.dot(step_rows, summing, precision=lax.Precision.HIGHEST, preferred_element_type=F32)

        own[1].wait()
        own[2].wait()
        landed(write.at[:, sib_tok, :], pair_recv.at[1])
        landed(read.at[:, sib_tok, :], pair_recv.at[2])
        for g in range(core_groups):
            scores[g] = jnp.where(allowed, dot_nt(read[g], write[g]), 0.0).astype(BF16)

        for j in range(half):
            landed(gains.at[j], gain_recv.at[j])
            decay[j * heads_dev : (j + 1) * heads_dev, :] = gains[j, 0:heads_dev, :]
        within = -decay[:, 0:1] * running
        grow = jnp.exp(within)
        shrink = step_rows * jnp.exp(-within)
        total = grow[:, SPAN - 1 : SPAN]
        factor = total * joined

        right_copies, above_copies, ahead_copies = [], [], []
        for g in range(core_groups):
            part = pl.ds(g * group_rows, group_rows)
            for copies, dst, send_sem, recv_sem, step in (
                (right_copies, right, right_send_sem, right_recv, 2),
                (above_copies, above, above_send, above_recv, 2),
                (ahead_copies, ahead, ahead_send, ahead_recv, 4),
            ):
                copies.append(pltpu.make_async_remote_copy(
                    src_ref=right_send.at[part, :], dst_ref=dst.at[part, :],
                    send_sem=send_sem.at[g], recv_sem=recv_sem.at[g],
                    device_id=(section, me - step), device_id_type=MESH,
                ))
        factor_copy = pltpu.make_async_remote_copy(
            src_ref=factor_send, dst_ref=above_factor, send_sem=factor_sem.at[0], recv_sem=factor_sem.at[1],
            device_id=(section, me - 2), device_id_type=MESH,
        )

        def hand_on(g):
            @pl.when(span > 1)
            def _():
                ahead_copies[g].start()

            right_copies[g].start()

        @pl.when(follows & (span > 0))
        def _():
            factor_send[...] = jnp.broadcast_to(factor, factor_send.shape)
            factor_copy.start()

        for g in reversed(range(core_groups)):
            for j in range(g * group_devs, (g + 1) * group_devs):
                landed(grad.at[pl.ds(j * rows, rows), :], grad_recv.at[j])
                for i in range(heads_dev):
                    head = j * heads_dev + i
                    part = pl.ds(head * width, width)
                    grown = grad[part, :].astype(F32) * grow[head : head + 1, :]
                    scaled[part, :] = grown.astype(BF16)
                    kept_scaled[part, :] = (grown * kept).astype(BF16)
            part = pl.ds(g * group_rows, group_rows)
            local_state[part, :] = dot_nn(kept_scaled[part, :], read[g])

            @pl.when(span == last_span)
            def _():
                right[part, :] = jnp.zeros((group_rows, right.shape[1]), BF16)
                if spans > 1:
                    right_send[part, :] = local_state[part, :].astype(BF16)
                    hand_on(g)

            @pl.when(follows & (span > 0))
            def _():
                right_send[part, :] = local_state[part, :].astype(BF16)
                above_copies[g].start()

        for g in range(core_groups):
            part = pl.ds(g * group_rows, group_rows)
            inner[part, :] = dot_nn(scaled[part, :], scores[g])

        for g in reversed(range(core_groups)):
            part = pl.ds(g * group_rows, group_rows)

            @pl.when(follows)
            def _():
                landed(right.at[part, :], right_recv.at[g])

            @pl.when(leads & (span < last_span))
            def _():
                if g == core_groups - 1:
                    landed(above_factor, factor_sem.at[1])
                landed(above.at[part, :], above_recv.at[g])
                landed(ahead.at[part, :], ahead_recv.at[g])
                for h in range(g * group_heads, (g + 1) * group_heads):
                    piece = pl.ds(h * width, width)
                    state = above[piece, :].astype(F32) + above_factor[h : h + 1, 0:1] * ahead[piece, :].astype(F32)
                    right[piece, :] = state.astype(BF16)
                    right_send[piece, :] = (local_state[piece, :] + factor[h : h + 1, :] * state).astype(BF16)

                @pl.when(span > 0)
                def _():
                    hand_on(g)

        res_copies = []
        for g in reversed(range(core_groups)):
            part = pl.ds(g * group_rows, group_rows)
            carried = dot_nt(right[part, :], write[g])
            for j in range(g * group_devs, (g + 1) * group_devs):
                for i in range(heads_dev):
                    head = j * heads_dev + i
                    piece = pl.ds(head * width, width)
                    first = (head - g * group_heads) * width
                    reach = end_match * total[head : head + 1, :]
                    result[piece, :] = (
                        shrink[head : head + 1, :] * (inner[piece, :] + reach * carried[first : first + width, :])
                        + gains[j, heads_dev + i : heads_dev + i + 1, 0:1] * grad[piece, :].astype(F32)
                    ).astype(BF16)
                copy = pltpu.make_async_remote_copy(
                    src_ref=result.at[pl.ds(j * rows, rows), :], dst_ref=res_ref.at[0, :, pl.ds(base, SPAN)],
                    send_sem=res_send.at[j], recv_sem=res_recv.at[span],
                    device_id=(section - 1, device_of(j)), device_id_type=MESH,
                )
                copy.start()
                res_copies.append(copy)

        for there, grad_copy, gain_copy in sends:
            @pl.when(there)
            def _():
                grad_copy.wait_send()
                gain_copy.wait_send()
        for copy in pairs:
            copy.wait_send()

        @pl.when(leads & (span > 0))
        def _():
            for copy in right_copies:
                copy.wait_send()

        @pl.when(leads & (span > 1))
        def _():
            for copy in ahead_copies:
                copy.wait_send()

        @pl.when(follows & (span > 0))
        def _():
            for copy in above_copies:
                copy.wait_send()
            factor_copy.wait_send()

        for copy in res_copies:
            copy.wait_send()

    @pl.when(section < last_section)
    def _():
        for z in range(spans):
            landed(res_ref.at[0, :, pl.ds(z * SPAN, SPAN)], res_recv.at[z])

    @pl.when(section == last_section)
    def _():
        zero_copy.wait()


def solution(mesh):
    sections, devs = mesh.shape["section"], mesh.shape["seq"]
    placed = (
        P("section", "seq", None),
        P("section", None, "seq"),
        P("section", "seq"),
        P("section", "seq"),
        P("section", None, "seq", None),
        P("section", None, "seq", None),
        P("section", None),
    )

    def local(grad_out, step_sizes, decay_rate, skip_gain, state_in, state_out, segment_ids):
        rows, seqlen = grad_out.shape[1:]
        heads_dev = decay_rate.shape[1]
        groups, tok, state = state_in.shape[1:]
        half = devs // 2
        all_rows = half * rows
        core_heads = half * heads_dev
        core_groups = groups // 2
        gain_rows = -(-2 * heads_dev // 8) * 8
        dma = pltpu.SemaphoreType.DMA
        anywhere = pl.BlockSpec(memory_space=pl.ANY)
        by_core = (1, core_groups, 2, tok, state)
        return pl.pallas_call(
            functools.partial(kernel, sections, devs),
            out_shape=pltpu.VMEM(grad_out.shape, BF16),
            in_specs=[anywhere] * 7,
            out_specs=anywhere,
            scratch_shapes=[
                pltpu.SMEM(decay_rate.shape, F32),
                pltpu.SMEM(skip_gain.shape, F32),
                pltpu.VMEM(segment_ids.shape, jnp.int32),
                pltpu.VMEM((gain_rows, LANES), F32),
                pltpu.VMEM((half, gain_rows, LANES), F32),
                pltpu.VMEM((core_heads, LANES), F32),
                pltpu.VMEM((2 * core_heads, SPAN), F32),
                pltpu.VMEM((core_heads, SPAN), F32),
                pltpu.VMEM((core_groups, SPAN, state), BF16),
                pltpu.VMEM((core_groups, SPAN, state), BF16),
                pltpu.VMEM((all_rows, SPAN), BF16),
                pltpu.VMEM((all_rows, SPAN), BF16),
                pltpu.VMEM((all_rows, SPAN), BF16),
                pltpu.VMEM((core_groups, SPAN, SPAN), BF16),
                pltpu.VMEM((all_rows, SPAN), F32),
                pltpu.VMEM((all_rows, state), F32),
                pltpu.VMEM((all_rows, state), BF16),
                pltpu.VMEM((all_rows, state), BF16),
                pltpu.VMEM((all_rows, state), BF16),
                pltpu.VMEM((all_rows, state), BF16),
                pltpu.VMEM((core_heads, LANES), F32),
                pltpu.VMEM((core_heads, LANES), F32),
                pltpu.VMEM((all_rows, SPAN), BF16),
                pltpu.VMEM((rows, seqlen), BF16),
                dma((half,)), dma((half,)), dma((half,)), dma((half,)),
                dma((3,)), dma((3,)), dma((3,)),
                dma((core_groups,)), dma((core_groups,)), dma((core_groups,)),
                dma((core_groups,)), dma((core_groups,)), dma((core_groups,)), dma((2,)),
                dma((half,)), dma((half,)), dma, dma((3,)),
            ],
            compiler_params=pltpu.CompilerParams(
                collective_id=0, has_side_effects=True, vmem_limit_bytes=64 * MIB - MIB * 3 // 4 - 2 * rows * seqlen
            ),
        )(
            grad_out, step_sizes, decay_rate, skip_gain,
            state_in.reshape(by_core), state_out.reshape(by_core), segment_ids,
        )

    return jax.shard_map(
        local, mesh=mesh, in_specs=placed, out_specs=P("section", "seq", None), check_vma=False
    )
```

```python
import functools

import jax
import jax.numpy as jnp
from jax import lax
from jax.experimental import pallas as pl
from jax.experimental.pallas import tpu as pltpu
from jax.sharding import PartitionSpec as P

SPAN = 256
LANES = 128
MIB = 1024 * 1024
MESH = pl.DeviceIdType.MESH
F32, BF16 = jnp.float32, jnp.bfloat16


def dot_nt(a, b):
    return lax.dot_general(a, b, (((1,), (1,)), ((), ())), preferred_element_type=F32)


def dot_nn(a, b):
    return jnp.dot(a, b, preferred_element_type=F32)


def kernel(
    sections, devs,
    grad_ref, step_ref, decay_hbm, skip_hbm, in_ref, out_proj_ref, seg_hbm,
    res_ref,
    decay_ref, skip_ref, seg_ref, gains_send, gains, decay, all_steps, steps, write, read, grad, scaled, kept_scaled, inner, local_state,
    right, right_send, above, ahead, factor_send, above_factor, result, zeros,
    grad_send, grad_recv, gain_send, gain_recv, pair_send, pair_recv, own_sem, right_send_sem, right_recv,
    above_send, above_recv, ahead_send, ahead_recv, factor_sem,
    res_send, res_recv, zero_sem, small_sem,
):
    half = devs // 2
    spans = devs // 2
    rows, heads_dev = grad_ref.shape[1], decay_hbm.shape[1]
    width = rows // heads_dev
    tok = step_ref.shape[2]
    core_groups = in_ref.shape[1]
    groups = 2 * core_groups
    core_heads = half * heads_dev
    group_devs = devs // groups
    group_rows = group_devs * rows
    group_heads = group_devs * heads_dev

    section = lax.axis_index("section")
    me = lax.axis_index("seq")
    span = me // 2
    core = me % 2
    sibling = 2 * span + 1 - core
    own_group = me // group_devs
    owner_core = own_group % 2
    slot = own_group // 2 * group_devs + me % group_devs
    base = pl.multiple_of(span * SPAN, SPAN)
    last_section = sections - 1
    last_span = spans - 1
    leads = (last_span - span) % 2 == 0
    follows = jnp.logical_not(leads)
    barrier = pltpu.get_barrier_semaphore()

    def signal(sec, seq):
        pl.semaphore_signal(barrier, inc=1, device_id=(sec, seq), device_id_type=MESH)

    def device_of(j):
        return (2 * (j // group_devs) + core) * group_devs + j % group_devs

    def landed(region, sem):
        pltpu.make_async_copy(region, region, sem).wait()

    @pl.when(section > 0)
    def _():
        for j in range(half):
            source = device_of(j)

            @pl.when(source != me)
            def _():
                signal(section, source)

        signal(section, sibling)

        @pl.when(span < last_span)
        def _():
            signal(section, me + 2)

        @pl.when(leads & (span < last_span))
        def _():
            signal(section, me + 4)

    @pl.when(section < last_section)
    def _():
        for z in range(spans):
            signal(section + 1, 2 * z + owner_core)

    own_tok = pl.ds(pl.multiple_of(core * tok, tok), tok)
    sib_tok = pl.ds(pl.multiple_of((1 - core) * tok, tok), tok)
    zero_copy = pltpu.make_async_copy(zeros, res_ref.at[0], zero_sem)

    @pl.when(section == last_section)
    def _():
        zeros[...] = jnp.zeros_like(zeros)
        zero_copy.start()

    @pl.when(section > 0)
    def _():
        small = [
            pltpu.make_async_copy(decay_hbm, decay_ref, small_sem.at[0]),
            pltpu.make_async_copy(skip_hbm, skip_ref, small_sem.at[1]),
            pltpu.make_async_copy(seg_hbm, seg_ref, small_sem.at[2]),
        ]
        own = [
            pltpu.make_async_copy(step_ref.at[0], all_steps.at[:, own_tok], own_sem.at[0]),
            pltpu.make_async_copy(out_proj_ref.at[0, :, core], read.at[:, own_tok, :], own_sem.at[1]),
            pltpu.make_async_copy(in_ref.at[0, :, core], write.at[:, own_tok, :], own_sem.at[2]),
        ]
        for copy in small + own:
            copy.start()
        for copy in small:
            copy.wait()
        for i in range(heads_dev):
            gains_send[i : i + 1, :] = jnp.full((1, LANES), decay_ref[0, i], F32)
            gains_send[heads_dev + i : heads_dev + i + 1, :] = jnp.full((1, LANES), skip_ref[0, i], F32)

        to_self = (core == owner_core).astype(jnp.int32)
        after_first = (span > 0).astype(jnp.int32)
        hands_two = (leads & (span > 1)).astype(jnp.int32)
        pl.semaphore_wait(barrier, half - to_self + 1 + after_first + hands_two + half)

        sends = []
        grad_slot = pl.ds(pl.multiple_of(slot * rows, rows), rows)
        for z in reversed(range(spans)):
            target = 2 * z + owner_core
            there = target != me
            piece = grad_ref.at[0, :, pl.ds(z * SPAN, SPAN)]
            grad_copy = pltpu.make_async_remote_copy(
                src_ref=piece, dst_ref=grad.at[grad_slot, :], send_sem=grad_send.at[z], recv_sem=grad_recv.at[slot],
                device_id=(section, target), device_id_type=MESH,
            )
            gain_copy = pltpu.make_async_remote_copy(
                src_ref=gains_send, dst_ref=gains.at[slot], send_sem=gain_send.at[z], recv_sem=gain_recv.at[slot],
                device_id=(section, target), device_id_type=MESH,
            )

            @pl.when(there)
            def _():
                gain_copy.start()
                grad_copy.start()

            @pl.when(jnp.logical_not(there))
            def _():
                pltpu.make_async_copy(gains_send, gains.at[slot], gain_recv.at[slot]).start()
                pltpu.make_async_copy(piece, grad.at[grad_slot, :], grad_recv.at[slot]).start()

            sends.append((there, grad_copy, gain_copy))

        pairs = []
        for number, (src, dst) in enumerate((
            (step_ref.at[0], all_steps.at[:, own_tok]),
            (out_proj_ref.at[0, :, 1 - core], read.at[:, own_tok, :]),
            (in_ref.at[0, :, 1 - core], write.at[:, own_tok, :]),
        )):
            copy = pltpu.make_async_remote_copy(
                src_ref=src, dst_ref=dst, send_sem=pair_send.at[number], recv_sem=pair_recv.at[number],
                device_id=(section, sibling), device_id_type=MESH,
            )
            copy.start()
            pairs.append(copy)

        seg = seg_ref[0:1, pl.ds(base, SPAN)].astype(F32)
        before = pl.multiple_of(jnp.maximum(base - 128, 0), 128)
        prev_end = seg_ref[0:1, pl.ds(before, 128)].astype(F32)[:, 127:128]
        seg_end = seg[:, SPAN - 1 : SPAN]
        kept = (seg == prev_end).astype(F32)
        end_match = (seg == seg_end).astype(F32)
        joined = (seg_end == prev_end).astype(F32)
        t_index = lax.broadcasted_iota(jnp.int32, (SPAN, SPAN), 0)
        s_index = lax.broadcasted_iota(jnp.int32, (SPAN, SPAN), 1)
        summing = (t_index <= s_index).astype(F32)

        own[0].wait()
        landed(all_steps.at[:, sib_tok], pair_recv.at[0])
        for g in range(core_groups):
            even = 2 * g * group_heads
            odd = even + group_heads
            steps[g * group_heads : (g + 1) * group_heads, :] = jnp.where(
                core == 0, all_steps[even : even + group_heads, :], all_steps[odd : odd + group_heads, :]
            )
        step_rows = steps[...]
        running = jnp.dot(step_rows, summing, precision=lax.Precision.HIGHEST, preferred_element_type=F32)

        for j in range(half):
            landed(gains.at[j], gain_recv.at[j])
            decay[j * heads_dev : (j + 1) * heads_dev, :] = gains[j, 0:heads_dev, :]
        within = -decay[:, 0:1] * running
        grow = jnp.exp(within)
        shrink = step_rows * jnp.exp(-within)
        total = grow[:, SPAN - 1 : SPAN]
        factor = total * joined

        right_copies, above_copies, ahead_copies = [], [], []
        for g in range(core_groups):
            part = pl.ds(g * group_rows, group_rows)
            for copies, dst, send_sem, recv_sem, step in (
                (right_copies, right, right_send_sem, right_recv, 2),
                (above_copies, above, above_send, above_recv, 2),
                (ahead_copies, ahead, ahead_send, ahead_recv, 4),
            ):
                copies.append(pltpu.make_async_remote_copy(
                    src_ref=right_send.at[part, :], dst_ref=dst.at[part, :],
                    send_sem=send_sem.at[g], recv_sem=recv_sem.at[g],
                    device_id=(section, me - step), device_id_type=MESH,
                ))
        factor_copy = pltpu.make_async_remote_copy(
            src_ref=factor_send, dst_ref=above_factor, send_sem=factor_sem.at[0], recv_sem=factor_sem.at[1],
            device_id=(section, me - 2), device_id_type=MESH,
        )

        def hand_on(g):
            @pl.when(span > 1)
            def _():
                ahead_copies[g].start()

            right_copies[g].start()

        @pl.when(follows & (span > 0))
        def _():
            factor_send[...] = jnp.broadcast_to(factor, factor_send.shape)
            factor_copy.start()

        own[1].wait()
        landed(read.at[:, sib_tok, :], pair_recv.at[1])
        for g in reversed(range(core_groups)):
            for j in range(g * group_devs, (g + 1) * group_devs):
                landed(grad.at[pl.ds(j * rows, rows), :], grad_recv.at[j])
                for i in range(heads_dev):
                    head = j * heads_dev + i
                    part = pl.ds(head * width, width)
                    grown = grad[part, :].astype(F32) * grow[head : head + 1, :]
                    scaled[part, :] = grown.astype(BF16)
                    kept_scaled[part, :] = (grown * kept).astype(BF16)
            part = pl.ds(g * group_rows, group_rows)
            local_state[part, :] = dot_nn(kept_scaled[part, :], read[g])

            @pl.when(span == last_span)
            def _():
                right[part, :] = jnp.zeros((group_rows, right.shape[1]), BF16)
                if spans > 1:
                    right_send[part, :] = local_state[part, :].astype(BF16)
                    hand_on(g)

            @pl.when(follows & (span > 0))
            def _():
                right_send[part, :] = local_state[part, :].astype(BF16)
                above_copies[g].start()

        own[2].wait()
        landed(write.at[:, sib_tok, :], pair_recv.at[2])
        seg_rows = jnp.broadcast_to(seg, (SPAN, SPAN))
        allowed = (t_index >= s_index) & (seg_rows == seg_rows.T)
        for g in range(core_groups):
            part = pl.ds(g * group_rows, group_rows)
            masked = jnp.where(allowed, dot_nt(read[g], write[g]), 0.0).astype(BF16)
            inner[part, :] = dot_nn(scaled[part, :], masked)

        for g in reversed(range(core_groups)):
            part = pl.ds(g * group_rows, group_rows)

            @pl.when(follows)
            def _():
                landed(right.at[part, :], right_recv.at[g])

            @pl.when(leads & (span < last_span))
            def _():
                if g == core_groups - 1:
                    landed(above_factor, factor_sem.at[1])
                landed(above.at[part, :], above_recv.at[g])
                landed(ahead.at[part, :], ahead_recv.at[g])
                for h in range(g * group_heads, (g + 1) * group_heads):
                    piece = pl.ds(h * width, width)
                    state = above[piece, :].astype(F32) + above_factor[h : h + 1, 0:1] * ahead[piece, :].astype(F32)
                    right[piece, :] = state.astype(BF16)
                    right_send[piece, :] = (local_state[piece, :] + factor[h : h + 1, :] * state).astype(BF16)

                @pl.when(span > 0)
                def _():
                    hand_on(g)

        res_copies = []
        for g in reversed(range(core_groups)):
            part = pl.ds(g * group_rows, group_rows)
            carried = dot_nt(right[part, :], write[g])
            for j in range(g * group_devs, (g + 1) * group_devs):
                for i in range(heads_dev):
                    head = j * heads_dev + i
                    piece = pl.ds(head * width, width)
                    first = (head - g * group_heads) * width
                    reach = end_match * total[head : head + 1, :]
                    result[piece, :] = (
                        shrink[head : head + 1, :] * (inner[piece, :] + reach * carried[first : first + width, :])
                        + gains[j, heads_dev + i : heads_dev + i + 1, 0:1] * grad[piece, :].astype(F32)
                    ).astype(BF16)
                copy = pltpu.make_async_remote_copy(
                    src_ref=result.at[pl.ds(j * rows, rows), :], dst_ref=res_ref.at[0, :, pl.ds(base, SPAN)],
                    send_sem=res_send.at[j], recv_sem=res_recv.at[span],
                    device_id=(section - 1, device_of(j)), device_id_type=MESH,
                )
                copy.start()
                res_copies.append(copy)

        for there, grad_copy, gain_copy in sends:
            @pl.when(there)
            def _():
                grad_copy.wait_send()
                gain_copy.wait_send()
        for copy in pairs:
            copy.wait_send()

        @pl.when(leads & (span > 0))
        def _():
            for copy in right_copies:
                copy.wait_send()

        @pl.when(leads & (span > 1))
        def _():
            for copy in ahead_copies:
                copy.wait_send()

        @pl.when(follows & (span > 0))
        def _():
            for copy in above_copies:
                copy.wait_send()
            factor_copy.wait_send()

        for copy in res_copies:
            copy.wait_send()

    @pl.when(section < last_section)
    def _():
        for z in range(spans):
            landed(res_ref.at[0, :, pl.ds(z * SPAN, SPAN)], res_recv.at[z])

    @pl.when(section == last_section)
    def _():
        zero_copy.wait()


def solution(mesh):
    sections, devs = mesh.shape["section"], mesh.shape["seq"]
    placed = (
        P("section", "seq", None),
        P("section", None, "seq"),
        P("section", "seq"),
        P("section", "seq"),
        P("section", None, "seq", None),
        P("section", None, "seq", None),
        P("section", None),
    )

    def local(grad_out, step_sizes, decay_rate, skip_gain, state_in, state_out, segment_ids):
        rows, seqlen = grad_out.shape[1:]
        heads_dev = decay_rate.shape[1]
        groups, tok, state = state_in.shape[1:]
        half = devs // 2
        all_rows = half * rows
        core_heads = half * heads_dev
        core_groups = groups // 2
        gain_rows = -(-2 * heads_dev // 8) * 8
        dma = pltpu.SemaphoreType.DMA
        anywhere = pl.BlockSpec(memory_space=pl.ANY)
        by_core = (1, core_groups, 2, tok, state)
        return pl.pallas_call(
            functools.partial(kernel, sections, devs),
            out_shape=pltpu.VMEM(grad_out.shape, BF16),
            in_specs=[anywhere] * 7,
            out_specs=anywhere,
            scratch_shapes=[
                pltpu.SMEM(decay_rate.shape, F32),
                pltpu.SMEM(skip_gain.shape, F32),
                pltpu.VMEM(segment_ids.shape, jnp.int32),
                pltpu.VMEM((gain_rows, LANES), F32),
                pltpu.VMEM((half, gain_rows, LANES), F32),
                pltpu.VMEM((core_heads, LANES), F32),
                pltpu.VMEM((2 * core_heads, SPAN), F32),
                pltpu.VMEM((core_heads, SPAN), F32),
                pltpu.VMEM((core_groups, SPAN, state), BF16),
                pltpu.VMEM((core_groups, SPAN, state), BF16),
                pltpu.VMEM((all_rows, SPAN), BF16),
                pltpu.VMEM((all_rows, SPAN), BF16),
                pltpu.VMEM((all_rows, SPAN), BF16),
                pltpu.VMEM((all_rows, SPAN), F32),
                pltpu.VMEM((all_rows, state), F32),
                pltpu.VMEM((all_rows, state), BF16),
                pltpu.VMEM((all_rows, state), BF16),
                pltpu.VMEM((all_rows, state), BF16),
                pltpu.VMEM((all_rows, state), BF16),
                pltpu.VMEM((core_heads, LANES), F32),
                pltpu.VMEM((core_heads, LANES), F32),
                pltpu.VMEM((all_rows, SPAN), BF16),
                pltpu.VMEM((rows, seqlen), BF16),
                dma((half,)), dma((half,)), dma((half,)), dma((half,)),
                dma((3,)), dma((3,)), dma((3,)),
                dma((core_groups,)), dma((core_groups,)), dma((core_groups,)),
                dma((core_groups,)), dma((core_groups,)), dma((core_groups,)), dma((2,)),
                dma((half,)), dma((half,)), dma, dma((3,)),
            ],
            compiler_params=pltpu.CompilerParams(
                collective_id=0, has_side_effects=True, vmem_limit_bytes=64 * MIB - MIB * 3 // 4 - 2 * rows * seqlen
            ),
        )(
            grad_out, step_sizes, decay_rate, skip_gain,
            state_in.reshape(by_core), state_out.reshape(by_core), segment_ids,
        )

    return jax.shard_map(
        local, mesh=mesh, in_specs=placed, out_specs=P("section", "seq", None), check_vma=False
    )
```

```python
import functools

import jax
import jax.numpy as jnp
from jax import lax
from jax.experimental import pallas as pl
from jax.experimental.pallas import tpu as pltpu
from jax.sharding import PartitionSpec as P

SPAN = 256
LANES = 128
MIB = 1024 * 1024


def group_counts(groups):
    few = 3 * groups // 8
    return few, groups - few
MESH = pl.DeviceIdType.MESH
F32, BF16 = jnp.float32, jnp.bfloat16


def dot_nt(a, b):
    return lax.dot_general(a, b, (((1,), (1,)), ((), ())), preferred_element_type=F32)


def dot_nn(a, b):
    return jnp.dot(a, b, preferred_element_type=F32)


def kernel(
    sections, devs,
    grad_ref, step_ref, decay_hbm, skip_hbm, in_ref, out_proj_ref, seg_hbm,
    res_ref,
    decay_ref, skip_ref, seg_ref, gains_send, gains, decay, all_steps, steps, write, read, grad, scaled, kept_scaled, inner, local_state,
    right, right_send, above, ahead, factor_send, above_factor, result, zeros,
    grad_send, grad_recv, gain_send, gain_recv, pair_send, pair_recv, own_sem, right_send_sem, right_recv,
    above_send, above_recv, ahead_send, ahead_recv, factor_sem,
    res_send, res_recv, zero_sem, small_sem,
):
    half = devs // 2
    spans = devs // 2
    rows, heads_dev = grad_ref.shape[1], decay_hbm.shape[1]
    width = rows // heads_dev
    tok = step_ref.shape[2]
    groups = in_ref.shape[1]
    counts = few, core_groups = group_counts(groups)
    firsts = core_groups, 0
    group_devs = devs // groups
    group_rows = group_devs * rows
    group_heads = group_devs * heads_dev

    section = lax.axis_index("section")
    me = lax.axis_index("seq")
    span = me // 2
    core = me % 2
    sibling = 2 * span + 1 - core
    own_group = me // group_devs
    owner_core = (own_group < core_groups).astype(jnp.int32)
    slot = me - (1 - owner_core) * core_groups * group_devs
    my_first = (1 - core) * core_groups
    my_count = few + core * (core_groups - few)
    base = pl.multiple_of(span * SPAN, SPAN)
    last_section = sections - 1
    last_span = spans - 1
    leads = (last_span - span) % 2 == 0
    follows = jnp.logical_not(leads)
    barrier = pltpu.get_barrier_semaphore()

    def signal(sec, seq):
        pl.semaphore_signal(barrier, inc=1, device_id=(sec, seq), device_id_type=MESH)

    def device_of(j):
        return my_first * group_devs + j

    def each_group(body):
        for g in reversed(range(core_groups)):
            if g < few:
                body(g)
            else:
                pl.when(g < my_count)(functools.partial(body, g))

    def on_core(body):
        for c in range(2):
            pl.when(core == c)(functools.partial(body, c))

    def landed(region, sem):
        pltpu.make_async_copy(region, region, sem).wait()

    @pl.when(section > 0)
    def _():
        def greet(g):
            for j in range(g * group_devs, (g + 1) * group_devs):
                source = device_of(j)

                @pl.when(source != me)
                def _():
                    signal(section, source)

        each_group(greet)
        signal(section, sibling)

        @pl.when(span < last_span)
        def _():
            signal(section, me + 2)

        @pl.when(leads & (span < last_span))
        def _():
            signal(section, me + 4)

    @pl.when(section < last_section)
    def _():
        for z in range(spans):
            signal(section + 1, 2 * z + owner_core)

    own_tok = pl.ds(pl.multiple_of(core * tok, tok), tok)
    sib_tok = pl.ds(pl.multiple_of((1 - core) * tok, tok), tok)
    zero_copy = pltpu.make_async_copy(zeros, res_ref.at[0], zero_sem)

    @pl.when(section == last_section)
    def _():
        zeros[...] = jnp.zeros_like(zeros)
        zero_copy.start()

    @pl.when(section > 0)
    def _():
        small = [
            pltpu.make_async_copy(decay_hbm, decay_ref, small_sem.at[0]),
            pltpu.make_async_copy(skip_hbm, skip_ref, small_sem.at[1]),
            pltpu.make_async_copy(seg_hbm, seg_ref, small_sem.at[2]),
        ]
        own_steps = pltpu.make_async_copy(step_ref.at[0], all_steps.at[:, own_tok], own_sem.at[0])

        def own_copies(c):
            mine, kept_at = pl.ds(firsts[c], counts[c]), pl.ds(0, counts[c])
            return (
                pltpu.make_async_copy(out_proj_ref.at[0, mine], read.at[kept_at, own_tok, :], own_sem.at[1]),
                pltpu.make_async_copy(in_ref.at[0, mine], write.at[kept_at, own_tok, :], own_sem.at[2]),
            )

        @on_core
        def _(c):
            for copy in own_copies(c):
                copy.start()

        decay[...] = jnp.zeros_like(decay)
        for copy in small + [own_steps]:
            copy.start()
        for copy in small:
            copy.wait()
        for i in range(heads_dev):
            gains_send[i : i + 1, :] = jnp.full((1, LANES), decay_ref[0, i], F32)
            gains_send[heads_dev + i : heads_dev + i + 1, :] = jnp.full((1, LANES), skip_ref[0, i], F32)

        to_self = (core == owner_core).astype(jnp.int32)
        after_first = (span > 0).astype(jnp.int32)
        hands_two = (leads & (span > 1)).astype(jnp.int32)
        pl.semaphore_wait(barrier, half - to_self + 1 + after_first + hands_two + my_count * group_devs)

        sends = []
        grad_slot = pl.ds(pl.multiple_of(slot * rows, rows), rows)
        for z in reversed(range(spans)):
            target = 2 * z + owner_core
            there = target != me
            piece = grad_ref.at[0, :, pl.ds(z * SPAN, SPAN)]
            grad_copy = pltpu.make_async_remote_copy(
                src_ref=piece, dst_ref=grad.at[grad_slot, :], send_sem=grad_send.at[z], recv_sem=grad_recv.at[slot],
                device_id=(section, target), device_id_type=MESH,
            )
            gain_copy = pltpu.make_async_remote_copy(
                src_ref=gains_send, dst_ref=gains.at[slot], send_sem=gain_send.at[z], recv_sem=gain_recv.at[slot],
                device_id=(section, target), device_id_type=MESH,
            )

            @pl.when(there)
            def _():
                gain_copy.start()
                grad_copy.start()

            @pl.when(jnp.logical_not(there))
            def _():
                pltpu.make_async_copy(gains_send, gains.at[slot], gain_recv.at[slot]).start()
                pltpu.make_async_copy(piece, grad.at[grad_slot, :], grad_recv.at[slot]).start()

            sends.append((there, grad_copy, gain_copy))

        def pair_copies(c):
            theirs, kept_at = pl.ds(firsts[1 - c], counts[1 - c]), pl.ds(0, counts[1 - c])
            return [
                pltpu.make_async_remote_copy(
                    src_ref=src, dst_ref=dst, send_sem=pair_send.at[number], recv_sem=pair_recv.at[number],
                    device_id=(section, sibling), device_id_type=MESH,
                )
                for number, (src, dst) in enumerate((
                    (step_ref.at[0], all_steps.at[:, own_tok]),
                    (out_proj_ref.at[0, theirs], read.at[kept_at, own_tok, :]),
                    (in_ref.at[0, theirs], write.at[kept_at, own_tok, :]),
                ))
            ]

        @on_core
        def _(c):
            for copy in pair_copies(c):
                copy.start()

        seg = seg_ref[0:1, pl.ds(base, SPAN)].astype(F32)
        before = pl.multiple_of(jnp.maximum(base - 128, 0), 128)
        prev_end = seg_ref[0:1, pl.ds(before, 128)].astype(F32)[:, 127:128]
        seg_end = seg[:, SPAN - 1 : SPAN]
        kept = (seg == prev_end).astype(F32)
        end_match = (seg == seg_end).astype(F32)
        joined = (seg_end == prev_end).astype(F32)
        t_index = lax.broadcasted_iota(jnp.int32, (SPAN, SPAN), 0)
        s_index = lax.broadcasted_iota(jnp.int32, (SPAN, SPAN), 1)
        summing = (t_index <= s_index).astype(F32)

        own_steps.wait()
        landed(all_steps.at[:, sib_tok], pair_recv.at[0])
        for g in range(core_groups):
            heads = all_steps[g * group_heads : (g + 1) * group_heads, :]
            if g < few:
                other = (core_groups + g) * group_heads
                heads = jnp.where(core == 0, all_steps[other : other + group_heads, :], heads)
            steps[g * group_heads : (g + 1) * group_heads, :] = heads
        step_rows = steps[...]
        running = jnp.dot(step_rows, summing, precision=lax.Precision.HIGHEST, preferred_element_type=F32)

        @each_group
        def _(g):
            for j in range(g * group_devs, (g + 1) * group_devs):
                landed(gains.at[j], gain_recv.at[j])
                decay[j * heads_dev : (j + 1) * heads_dev, :] = gains[j, 0:heads_dev, :]

        within = -decay[:, 0:1] * running
        grow = jnp.exp(within)
        shrink = step_rows * jnp.exp(-within)
        total = grow[:, SPAN - 1 : SPAN]
        factor = total * joined

        right_copies, above_copies, ahead_copies = [], [], []
        for g in range(core_groups):
            part = pl.ds(g * group_rows, group_rows)
            for copies, dst, send_sem, recv_sem, step in (
                (right_copies, right, right_send_sem, right_recv, 2),
                (above_copies, above, above_send, above_recv, 2),
                (ahead_copies, ahead, ahead_send, ahead_recv, 4),
            ):
                copies.append(pltpu.make_async_remote_copy(
                    src_ref=right_send.at[part, :], dst_ref=dst.at[part, :],
                    send_sem=send_sem.at[g], recv_sem=recv_sem.at[g],
                    device_id=(section, me - step), device_id_type=MESH,
                ))
        factor_copy = pltpu.make_async_remote_copy(
            src_ref=factor_send, dst_ref=above_factor, send_sem=factor_sem.at[0], recv_sem=factor_sem.at[1],
            device_id=(section, me - 2), device_id_type=MESH,
        )

        def hand_on(g):
            @pl.when(span > 1)
            def _():
                ahead_copies[g].start()

            right_copies[g].start()

        @pl.when(follows & (span > 0))
        def _():
            factor_send[...] = jnp.broadcast_to(factor, factor_send.shape)
            factor_copy.start()

        @on_core
        def _(c):
            own_copies(c)[0].wait()
            landed(read.at[pl.ds(0, counts[c]), sib_tok, :], pair_recv.at[1])

        @each_group
        def _(g):
            for j in range(g * group_devs, (g + 1) * group_devs):
                landed(grad.at[pl.ds(j * rows, rows), :], grad_recv.at[j])
                for i in range(heads_dev):
                    head = j * heads_dev + i
                    part = pl.ds(head * width, width)
                    grown = grad[part, :].astype(F32) * grow[head : head + 1, :]
                    scaled[part, :] = grown.astype(BF16)
                    kept_scaled[part, :] = (grown * kept).astype(BF16)
            part = pl.ds(g * group_rows, group_rows)
            local_state[part, :] = dot_nn(kept_scaled[part, :], read[g])

            @pl.when(span == last_span)
            def _():
                right[part, :] = jnp.zeros((group_rows, right.shape[1]), BF16)
                if spans > 1:
                    right_send[part, :] = local_state[part, :].astype(BF16)
                    hand_on(g)

            @pl.when(follows & (span > 0))
            def _():
                right_send[part, :] = local_state[part, :].astype(BF16)
                above_copies[g].start()

        @on_core
        def _(c):
            own_copies(c)[1].wait()
            landed(write.at[pl.ds(0, counts[c]), sib_tok, :], pair_recv.at[2])

        seg_rows = jnp.broadcast_to(seg, (SPAN, SPAN))
        allowed = (t_index >= s_index) & (seg_rows == seg_rows.T)

        @each_group
        def _(g):
            part = pl.ds(g * group_rows, group_rows)
            masked = jnp.where(allowed, dot_nt(read[g], write[g]), 0.0).astype(BF16)
            inner[part, :] = dot_nn(scaled[part, :], masked)

        @pl.when(leads & (span < last_span))
        def _():
            landed(above_factor, factor_sem.at[1])

        @each_group
        def _(g):
            part = pl.ds(g * group_rows, group_rows)

            @pl.when(follows)
            def _():
                landed(right.at[part, :], right_recv.at[g])

            @pl.when(leads & (span < last_span))
            def _():
                landed(above.at[part, :], above_recv.at[g])
                landed(ahead.at[part, :], ahead_recv.at[g])
                for h in range(g * group_heads, (g + 1) * group_heads):
                    piece = pl.ds(h * width, width)
                    state = above[piece, :].astype(F32) + above_factor[h : h + 1, 0:1] * ahead[piece, :].astype(F32)
                    right[piece, :] = state.astype(BF16)
                    right_send[piece, :] = (local_state[piece, :] + factor[h : h + 1, :] * state).astype(BF16)

                @pl.when(span > 0)
                def _():
                    hand_on(g)

        def res_copy(j):
            return pltpu.make_async_remote_copy(
                src_ref=result.at[pl.ds(j * rows, rows), :], dst_ref=res_ref.at[0, :, pl.ds(base, SPAN)],
                send_sem=res_send.at[j], recv_sem=res_recv.at[span],
                device_id=(section - 1, device_of(j)), device_id_type=MESH,
            )

        @each_group
        def _(g):
            part = pl.ds(g * group_rows, group_rows)
            carried = dot_nt(right[part, :], write[g])
            for j in range(g * group_devs, (g + 1) * group_devs):
                for i in range(heads_dev):
                    head = j * heads_dev + i
                    piece = pl.ds(head * width, width)
                    first = (head - g * group_heads) * width
                    reach = end_match * total[head : head + 1, :]
                    result[piece, :] = (
                        shrink[head : head + 1, :] * (inner[piece, :] + reach * carried[first : first + width, :])
                        + gains[j, heads_dev + i : heads_dev + i + 1, 0:1] * grad[piece, :].astype(F32)
                    ).astype(BF16)
                res_copy(j).start()

        for there, grad_copy, gain_copy in sends:
            @pl.when(there)
            def _():
                grad_copy.wait_send()
                gain_copy.wait_send()

        @on_core
        def _(c):
            for copy in pair_copies(c):
                copy.wait_send()

        @pl.when(follows & (span > 0))
        def _():
            factor_copy.wait_send()

        @each_group
        def _(g):
            @pl.when(leads & (span > 0))
            def _():
                right_copies[g].wait_send()

            @pl.when(leads & (span > 1))
            def _():
                ahead_copies[g].wait_send()

            @pl.when(follows & (span > 0))
            def _():
                above_copies[g].wait_send()

            for j in range(g * group_devs, (g + 1) * group_devs):
                res_copy(j).wait_send()

    @pl.when(section < last_section)
    def _():
        for z in range(spans):
            landed(res_ref.at[0, :, pl.ds(z * SPAN, SPAN)], res_recv.at[z])

    @pl.when(section == last_section)
    def _():
        zero_copy.wait()


def solution(mesh):
    sections, devs = mesh.shape["section"], mesh.shape["seq"]
    placed = (
        P("section", "seq", None),
        P("section", None, "seq"),
        P("section", "seq"),
        P("section", "seq"),
        P("section", None, "seq", None),
        P("section", None, "seq", None),
        P("section", None),
    )

    def local(grad_out, step_sizes, decay_rate, skip_gain, state_in, state_out, segment_ids):
        rows, seqlen = grad_out.shape[1:]
        heads_dev = decay_rate.shape[1]
        groups, _, state = state_in.shape[1:]
        half = devs // 2
        core_groups = group_counts(groups)[1]
        slots = core_groups * (devs // groups)
        all_rows = slots * rows
        core_heads = slots * heads_dev
        gain_rows = -(-2 * heads_dev // 8) * 8
        dma = pltpu.SemaphoreType.DMA
        anywhere = pl.BlockSpec(memory_space=pl.ANY)
        return pl.pallas_call(
            functools.partial(kernel, sections, devs),
            out_shape=pltpu.VMEM(grad_out.shape, BF16),
            in_specs=[anywhere] * 7,
            out_specs=anywhere,
            scratch_shapes=[
                pltpu.SMEM(decay_rate.shape, F32),
                pltpu.SMEM(skip_gain.shape, F32),
                pltpu.VMEM(segment_ids.shape, jnp.int32),
                pltpu.VMEM((gain_rows, LANES), F32),
                pltpu.VMEM((slots, gain_rows, LANES), F32),
                pltpu.VMEM((core_heads, LANES), F32),
                pltpu.VMEM((step_sizes.shape[1], SPAN), F32),
                pltpu.VMEM((core_heads, SPAN), F32),
                pltpu.VMEM((core_groups, SPAN, state), BF16),
                pltpu.VMEM((core_groups, SPAN, state), BF16),
                pltpu.VMEM((all_rows, SPAN), BF16),
                pltpu.VMEM((all_rows, SPAN), BF16),
                pltpu.VMEM((all_rows, SPAN), BF16),
                pltpu.VMEM((all_rows, SPAN), F32),
                pltpu.VMEM((all_rows, state), F32),
                pltpu.VMEM((all_rows, state), BF16),
                pltpu.VMEM((all_rows, state), BF16),
                pltpu.VMEM((all_rows, state), BF16),
                pltpu.VMEM((all_rows, state), BF16),
                pltpu.VMEM((core_heads, LANES), F32),
                pltpu.VMEM((core_heads, LANES), F32),
                pltpu.VMEM((all_rows, SPAN), BF16),
                pltpu.VMEM((rows, seqlen), BF16),
                dma((half,)), dma((slots,)), dma((half,)), dma((slots,)),
                dma((3,)), dma((3,)), dma((3,)),
                dma((core_groups,)), dma((core_groups,)), dma((core_groups,)),
                dma((core_groups,)), dma((core_groups,)), dma((core_groups,)), dma((2,)),
                dma((slots,)), dma((half,)), dma, dma((3,)),
            ],
            compiler_params=pltpu.CompilerParams(
                collective_id=0, has_side_effects=True, vmem_limit_bytes=64 * MIB - MIB * 3 // 4 - 2 * rows * seqlen
            ),
        )(
            grad_out, step_sizes, decay_rate, skip_gain,
            state_in, state_out, segment_ids,
        )

    return jax.shard_map(
        local, mesh=mesh, in_specs=placed, out_specs=P("section", "seq", None), check_vma=False
    )
```

```python
import functools

import jax
import jax.numpy as jnp
from jax import lax
from jax.experimental import pallas as pl
from jax.experimental.pallas import tpu as pltpu
from jax.sharding import PartitionSpec as P

SPAN = 256
LANES = 128
MIB = 1024 * 1024


def group_counts(groups):
    few = 3 * groups // 8
    return few, groups - few
MESH = pl.DeviceIdType.MESH
F32, BF16 = jnp.float32, jnp.bfloat16


def dot_nt(a, b):
    return lax.dot_general(a, b, (((1,), (1,)), ((), ())), preferred_element_type=F32)


def dot_nn(a, b):
    return jnp.dot(a, b, preferred_element_type=F32)


def kernel(
    sections, devs,
    grad_ref, step_ref, decay_hbm, skip_hbm, in_ref, out_proj_ref, seg_hbm,
    res_ref,
    decay_ref, skip_ref, seg_ref, gains_send, gains, decay, all_steps, steps, write, read, grad, scaled, kept_scaled, inner, local_state,
    right, right_send, above, ahead, factor_send, above_factor, result, zeros,
    grad_send, grad_recv, gain_send, gain_recv, pair_send, pair_recv, own_sem, right_send_sem, right_recv,
    above_send, above_recv, ahead_send, ahead_recv, factor_sem,
    res_send, res_recv, zero_sem, small_sem,
):
    half = devs // 2
    spans = devs // 2
    rows, heads_dev = grad_ref.shape[1], decay_hbm.shape[1]
    width = rows // heads_dev
    tok = step_ref.shape[2]
    groups = in_ref.shape[1]
    counts = few, core_groups = group_counts(groups)
    firsts = core_groups, 0
    group_devs = devs // groups
    group_rows = group_devs * rows
    group_heads = group_devs * heads_dev

    section = lax.axis_index("section")
    me = lax.axis_index("seq")
    span = me // 2
    core = me % 2
    sibling = 2 * span + 1 - core
    own_group = me // group_devs
    owner_core = (own_group < core_groups).astype(jnp.int32)
    slot = me - (1 - owner_core) * core_groups * group_devs
    my_first = (1 - core) * core_groups
    my_count = few + core * (core_groups - few)
    base = pl.multiple_of(span * SPAN, SPAN)
    last_section = sections - 1
    last_span = spans - 1
    leads = (last_span - span) % 2 == 0
    follows = jnp.logical_not(leads)
    barrier = pltpu.get_barrier_semaphore()

    def signal(sec, seq):
        pl.semaphore_signal(barrier, inc=1, device_id=(sec, seq), device_id_type=MESH)

    def device_of(j):
        return my_first * group_devs + j

    def each_group(body):
        for g in reversed(range(core_groups)):
            if g < few:
                body(g)
            else:
                pl.when(g < my_count)(functools.partial(body, g))

    def on_core(body):
        for c in range(2):
            pl.when(core == c)(functools.partial(body, c))

    def landed(region, sem):
        pltpu.make_async_copy(region, region, sem).wait()

    @pl.when(section > 0)
    def _():
        def greet(g):
            for j in range(g * group_devs, (g + 1) * group_devs):
                source = device_of(j)

                @pl.when(source != me)
                def _():
                    signal(section, source)

        each_group(greet)
        signal(section, sibling)

        @pl.when(span < last_span)
        def _():
            signal(section, me + 2)

        @pl.when(leads & (span < last_span))
        def _():
            signal(section, me + 4)

    @pl.when(section < last_section)
    def _():
        for z in range(spans):
            signal(section + 1, 2 * z + owner_core)

    own_tok = pl.ds(pl.multiple_of(core * tok, tok), tok)
    sib_tok = pl.ds(pl.multiple_of((1 - core) * tok, tok), tok)
    zero_copy = pltpu.make_async_copy(zeros, res_ref.at[0], zero_sem)

    @pl.when(section == last_section)
    def _():
        zeros[...] = jnp.zeros_like(zeros)
        zero_copy.start()

    @pl.when(section > 0)
    def _():
        small = [
            pltpu.make_async_copy(decay_hbm, decay_ref, small_sem.at[0]),
            pltpu.make_async_copy(skip_hbm, skip_ref, small_sem.at[1]),
            pltpu.make_async_copy(seg_hbm, seg_ref, small_sem.at[2]),
        ]
        own_steps = pltpu.make_async_copy(step_ref.at[0], all_steps.at[:, own_tok], own_sem.at[0])

        def own_copies(c):
            mine, kept_at = pl.ds(firsts[c], counts[c]), pl.ds(0, counts[c])
            return (
                pltpu.make_async_copy(out_proj_ref.at[0, mine], read.at[kept_at, own_tok, :], own_sem.at[1]),
                pltpu.make_async_copy(in_ref.at[0, mine], write.at[kept_at, own_tok, :], own_sem.at[2]),
            )

        @on_core
        def _(c):
            for copy in own_copies(c):
                copy.start()

        decay[...] = jnp.zeros_like(decay)
        for copy in small + [own_steps]:
            copy.start()
        to_self = (core == owner_core).astype(jnp.int32)
        after_first = (span > 0).astype(jnp.int32)
        hands_two = (leads & (span > 1)).astype(jnp.int32)
        pl.semaphore_wait(barrier, half - to_self + 1 + after_first + hands_two + my_count * group_devs)

        def pair_copies(c):
            theirs, kept_at = pl.ds(firsts[1 - c], counts[1 - c]), pl.ds(0, counts[1 - c])
            return [
                pltpu.make_async_remote_copy(
                    src_ref=src, dst_ref=dst, send_sem=pair_send.at[number], recv_sem=pair_recv.at[number],
                    device_id=(section, sibling), device_id_type=MESH,
                )
                for number, (src, dst) in enumerate((
                    (step_ref.at[0], all_steps.at[:, own_tok]),
                    (out_proj_ref.at[0, theirs], read.at[kept_at, own_tok, :]),
                    (in_ref.at[0, theirs], write.at[kept_at, own_tok, :]),
                ))
            ]

        @on_core
        def _(c):
            for copy in pair_copies(c)[:2]:
                copy.start()

        sends = []
        grad_slot = pl.ds(pl.multiple_of(slot * rows, rows), rows)
        for z in reversed(range(spans)):
            target = 2 * z + owner_core
            there = target != me
            piece = grad_ref.at[0, :, pl.ds(z * SPAN, SPAN)]
            grad_copy = pltpu.make_async_remote_copy(
                src_ref=piece, dst_ref=grad.at[grad_slot, :], send_sem=grad_send.at[z], recv_sem=grad_recv.at[slot],
                device_id=(section, target), device_id_type=MESH,
            )
            gain_copy = pltpu.make_async_remote_copy(
                src_ref=gains_send, dst_ref=gains.at[slot], send_sem=gain_send.at[z], recv_sem=gain_recv.at[slot],
                device_id=(section, target), device_id_type=MESH,
            )

            @pl.when(there)
            def _():
                grad_copy.start()

            @pl.when(jnp.logical_not(there))
            def _():
                pltpu.make_async_copy(piece, grad.at[grad_slot, :], grad_recv.at[slot]).start()

            sends.append((there, grad_copy, gain_copy))

        for copy in small:
            copy.wait()
        for i in range(heads_dev):
            gains_send[i : i + 1, :] = jnp.full((1, LANES), decay_ref[0, i], F32)
            gains_send[heads_dev + i : heads_dev + i + 1, :] = jnp.full((1, LANES), skip_ref[0, i], F32)

        for there, _, gain_copy in sends:
            pl.when(there)(gain_copy.start)

            @pl.when(jnp.logical_not(there))
            def _():
                pltpu.make_async_copy(gains_send, gains.at[slot], gain_recv.at[slot]).start()


        seg = seg_ref[0:1, pl.ds(base, SPAN)].astype(F32)
        before = pl.multiple_of(jnp.maximum(base - 128, 0), 128)
        prev_end = seg_ref[0:1, pl.ds(before, 128)].astype(F32)[:, 127:128]
        seg_end = seg[:, SPAN - 1 : SPAN]
        kept = (seg == prev_end).astype(F32)
        end_match = (seg == seg_end).astype(F32)
        joined = (seg_end == prev_end).astype(F32)
        t_index = lax.broadcasted_iota(jnp.int32, (SPAN, SPAN), 0)
        s_index = lax.broadcasted_iota(jnp.int32, (SPAN, SPAN), 1)
        summing = (t_index <= s_index).astype(F32)

        own_steps.wait()
        landed(all_steps.at[:, sib_tok], pair_recv.at[0])
        for g in range(core_groups):
            heads = all_steps[g * group_heads : (g + 1) * group_heads, :]
            if g < few:
                other = (core_groups + g) * group_heads
                heads = jnp.where(core == 0, all_steps[other : other + group_heads, :], heads)
            steps[g * group_heads : (g + 1) * group_heads, :] = heads
        step_rows = steps[...]
        running = jnp.dot(step_rows, summing, precision=lax.Precision.HIGHEST, preferred_element_type=F32)

        @each_group
        def _(g):
            for j in range(g * group_devs, (g + 1) * group_devs):
                landed(gains.at[j], gain_recv.at[j])
                decay[j * heads_dev : (j + 1) * heads_dev, :] = gains[j, 0:heads_dev, :]

        within = -decay[:, 0:1] * running
        grow = jnp.exp(within)
        shrink = step_rows * jnp.exp(-within)
        total = grow[:, SPAN - 1 : SPAN]
        factor = total * joined

        right_copies, above_copies, ahead_copies = [], [], []
        for g in range(core_groups):
            part = pl.ds(g * group_rows, group_rows)
            for copies, dst, send_sem, recv_sem, step in (
                (right_copies, right, right_send_sem, right_recv, 2),
                (above_copies, above, above_send, above_recv, 2),
                (ahead_copies, ahead, ahead_send, ahead_recv, 4),
            ):
                copies.append(pltpu.make_async_remote_copy(
                    src_ref=right_send.at[part, :], dst_ref=dst.at[part, :],
                    send_sem=send_sem.at[g], recv_sem=recv_sem.at[g],
                    device_id=(section, me - step), device_id_type=MESH,
                ))
        factor_copy = pltpu.make_async_remote_copy(
            src_ref=factor_send, dst_ref=above_factor, send_sem=factor_sem.at[0], recv_sem=factor_sem.at[1],
            device_id=(section, me - 2), device_id_type=MESH,
        )

        def hand_on(g):
            @pl.when(span > 1)
            def _():
                ahead_copies[g].start()

            @pl.when(span <= 1)
            def _():
                right_copies[g].start()

        @pl.when(follows & (span > 0))
        def _():
            factor_send[...] = jnp.broadcast_to(factor, factor_send.shape)
            factor_copy.start()

        @on_core
        def _(c):
            own_copies(c)[0].wait()
            landed(read.at[pl.ds(0, counts[c]), sib_tok, :], pair_recv.at[1])

        @each_group
        def _(g):
            for j in range(g * group_devs, (g + 1) * group_devs):
                landed(grad.at[pl.ds(j * rows, rows), :], grad_recv.at[j])
                for i in range(heads_dev):
                    head = j * heads_dev + i
                    part = pl.ds(head * width, width)
                    grown = grad[part, :].astype(F32) * grow[head : head + 1, :]
                    scaled[part, :] = grown.astype(BF16)
                    kept_scaled[part, :] = (grown * kept).astype(BF16)
            part = pl.ds(g * group_rows, group_rows)
            local_state[part, :] = dot_nn(kept_scaled[part, :], read[g])

            @pl.when(span == last_span)
            def _():
                right[part, :] = jnp.zeros((group_rows, right.shape[1]), BF16)
                if spans > 1:
                    right_send[part, :] = local_state[part, :].astype(BF16)
                    hand_on(g)

            @pl.when(follows & (span > 0))
            def _():
                right_send[part, :] = local_state[part, :].astype(BF16)
                above_copies[g].start()

        @pl.when((span == last_span) & (span > 1))
        def _():
            each_group(lambda g: right_copies[g].start())

        @on_core
        def _(c):
            pair_copies(c)[2].start()
            own_copies(c)[1].wait()
            landed(write.at[pl.ds(0, counts[c]), sib_tok, :], pair_recv.at[2])

        seg_rows = jnp.broadcast_to(seg, (SPAN, SPAN))
        allowed = (t_index >= s_index) & (seg_rows == seg_rows.T)

        @each_group
        def _(g):
            part = pl.ds(g * group_rows, group_rows)
            masked = jnp.where(allowed, dot_nt(read[g], write[g]), 0.0).astype(BF16)
            inner[part, :] = dot_nn(scaled[part, :], masked)

        @pl.when(leads & (span < last_span))
        def _():
            landed(above_factor, factor_sem.at[1])

        @each_group
        def _(g):
            part = pl.ds(g * group_rows, group_rows)

            @pl.when(follows)
            def _():
                landed(right.at[part, :], right_recv.at[g])

            @pl.when(leads & (span < last_span))
            def _():
                landed(above.at[part, :], above_recv.at[g])
                landed(ahead.at[part, :], ahead_recv.at[g])
                for h in range(g * group_heads, (g + 1) * group_heads):
                    piece = pl.ds(h * width, width)
                    state = above[piece, :].astype(F32) + above_factor[h : h + 1, 0:1] * ahead[piece, :].astype(F32)
                    right[piece, :] = state.astype(BF16)
                    right_send[piece, :] = (local_state[piece, :] + factor[h : h + 1, :] * state).astype(BF16)

                @pl.when(span > 0)
                def _():
                    hand_on(g)

        @pl.when(leads & (span < last_span) & (span > 1))
        def _():
            each_group(lambda g: right_copies[g].start())

        def res_copy(j):
            return pltpu.make_async_remote_copy(
                src_ref=result.at[pl.ds(j * rows, rows), :], dst_ref=res_ref.at[0, :, pl.ds(base, SPAN)],
                send_sem=res_send.at[j], recv_sem=res_recv.at[span],
                device_id=(section - 1, device_of(j)), device_id_type=MESH,
            )

        @each_group
        def _(g):
            part = pl.ds(g * group_rows, group_rows)
            carried = dot_nt(right[part, :], write[g])
            for j in range(g * group_devs, (g + 1) * group_devs):
                for i in range(heads_dev):
                    head = j * heads_dev + i
                    piece = pl.ds(head * width, width)
                    first = (head - g * group_heads) * width
                    reach = end_match * total[head : head + 1, :]
                    result[piece, :] = (
                        shrink[head : head + 1, :] * (inner[piece, :] + reach * carried[first : first + width, :])
                        + gains[j, heads_dev + i : heads_dev + i + 1, 0:1] * grad[piece, :].astype(F32)
                    ).astype(BF16)
                res_copy(j).start()

        for there, grad_copy, gain_copy in sends:
            @pl.when(there)
            def _():
                grad_copy.wait_send()
                gain_copy.wait_send()

        @on_core
        def _(c):
            for copy in pair_copies(c):
                copy.wait_send()

        @pl.when(follows & (span > 0))
        def _():
            factor_copy.wait_send()

        @each_group
        def _(g):
            @pl.when(leads & (span > 0))
            def _():
                right_copies[g].wait_send()

            @pl.when(leads & (span > 1))
            def _():
                ahead_copies[g].wait_send()

            @pl.when(follows & (span > 0))
            def _():
                above_copies[g].wait_send()

            for j in range(g * group_devs, (g + 1) * group_devs):
                res_copy(j).wait_send()

    @pl.when(section < last_section)
    def _():
        for z in range(spans):
            landed(res_ref.at[0, :, pl.ds(z * SPAN, SPAN)], res_recv.at[z])

    @pl.when(section == last_section)
    def _():
        zero_copy.wait()


def solution(mesh):
    sections, devs = mesh.shape["section"], mesh.shape["seq"]
    placed = (
        P("section", "seq", None),
        P("section", None, "seq"),
        P("section", "seq"),
        P("section", "seq"),
        P("section", None, "seq", None),
        P("section", None, "seq", None),
        P("section", None),
    )

    def local(grad_out, step_sizes, decay_rate, skip_gain, state_in, state_out, segment_ids):
        rows, seqlen = grad_out.shape[1:]
        heads_dev = decay_rate.shape[1]
        groups, _, state = state_in.shape[1:]
        half = devs // 2
        core_groups = group_counts(groups)[1]
        slots = core_groups * (devs // groups)
        all_rows = slots * rows
        core_heads = slots * heads_dev
        gain_rows = -(-2 * heads_dev // 8) * 8
        dma = pltpu.SemaphoreType.DMA
        anywhere = pl.BlockSpec(memory_space=pl.ANY)
        return pl.pallas_call(
            functools.partial(kernel, sections, devs),
            out_shape=pltpu.VMEM(grad_out.shape, BF16),
            in_specs=[anywhere] * 7,
            out_specs=anywhere,
            scratch_shapes=[
                pltpu.SMEM(decay_rate.shape, F32),
                pltpu.SMEM(skip_gain.shape, F32),
                pltpu.VMEM(segment_ids.shape, jnp.int32),
                pltpu.VMEM((gain_rows, LANES), F32),
                pltpu.VMEM((slots, gain_rows, LANES), F32),
                pltpu.VMEM((core_heads, LANES), F32),
                pltpu.VMEM((step_sizes.shape[1], SPAN), F32),
                pltpu.VMEM((core_heads, SPAN), F32),
                pltpu.VMEM((core_groups, SPAN, state), BF16),
                pltpu.VMEM((core_groups, SPAN, state), BF16),
                pltpu.VMEM((all_rows, SPAN), BF16),
                pltpu.VMEM((all_rows, SPAN), BF16),
                pltpu.VMEM((all_rows, SPAN), BF16),
                pltpu.VMEM((all_rows, SPAN), F32),
                pltpu.VMEM((all_rows, state), F32),
                pltpu.VMEM((all_rows, state), BF16),
                pltpu.VMEM((all_rows, state), BF16),
                pltpu.VMEM((all_rows, state), BF16),
                pltpu.VMEM((all_rows, state), BF16),
                pltpu.VMEM((core_heads, LANES), F32),
                pltpu.VMEM((core_heads, LANES), F32),
                pltpu.VMEM((all_rows, SPAN), BF16),
                pltpu.VMEM((rows, seqlen), BF16),
                dma((half,)), dma((slots,)), dma((half,)), dma((slots,)),
                dma((3,)), dma((3,)), dma((3,)),
                dma((core_groups,)), dma((core_groups,)), dma((core_groups,)),
                dma((core_groups,)), dma((core_groups,)), dma((core_groups,)), dma((2,)),
                dma((slots,)), dma((half,)), dma, dma((3,)),
            ],
            compiler_params=pltpu.CompilerParams(
                collective_id=0, has_side_effects=True, vmem_limit_bytes=64 * MIB - MIB * 3 // 4 - 2 * rows * seqlen
            ),
        )(
            grad_out, step_sizes, decay_rate, skip_gain,
            state_in, state_out, segment_ids,
        )

    return jax.shard_map(
        local, mesh=mesh, in_specs=placed, out_specs=P("section", "seq", None), check_vma=False
    )
```

```python
import functools

import jax
import jax.numpy as jnp
from jax import lax
from jax.experimental import pallas as pl
from jax.experimental.pallas import tpu as pltpu
from jax.sharding import PartitionSpec as P

SPAN = 256
LANES = 128
MIB = 1024 * 1024


def group_counts(groups):
    few = 3 * groups // 8
    return few, groups - few
MESH = pl.DeviceIdType.MESH
F32, BF16 = jnp.float32, jnp.bfloat16


def dot_nt(a, b):
    return lax.dot_general(a, b, (((1,), (1,)), ((), ())), preferred_element_type=F32)


def dot_nn(a, b):
    return jnp.dot(a, b, preferred_element_type=F32)


def kernel(
    sections, devs,
    grad_ref, step_ref, decay_hbm, skip_hbm, in_ref, out_proj_ref, seg_hbm,
    res_ref,
    decay_ref, skip_ref, seg_ref, gains_send, gains, decay, all_steps, steps, write, read, grad, scaled, kept_scaled, inner, local_state,
    right, right_send, above, ahead, factor_send, above_factor, result, zeros,
    grad_send, grad_recv, gain_send, gain_recv, pair_send, pair_recv, own_sem, right_send_sem, right_recv,
    above_send, above_recv, ahead_send, ahead_recv, factor_sem,
    res_send, res_recv, zero_sem, small_sem,
):
    half = devs // 2
    spans = devs // 2
    rows, heads_dev = grad_ref.shape[1], decay_hbm.shape[1]
    width = rows // heads_dev
    tok = step_ref.shape[2]
    groups = in_ref.shape[1]
    counts = few, core_groups = group_counts(groups)
    firsts = core_groups, 0
    group_devs = devs // groups
    group_rows = group_devs * rows
    group_heads = group_devs * heads_dev

    section = lax.axis_index("section")
    me = lax.axis_index("seq")
    span = me // 2
    core = me % 2
    sibling = 2 * span + 1 - core
    own_group = me // group_devs
    owner_core = (own_group < core_groups).astype(jnp.int32)
    slot = me - (1 - owner_core) * core_groups * group_devs
    my_first = (1 - core) * core_groups
    my_count = few + core * (core_groups - few)
    base = pl.multiple_of(span * SPAN, SPAN)
    last_section = sections - 1
    last_span = spans - 1
    leads = (last_span - span) % 2 == 0
    follows = jnp.logical_not(leads)
    barrier = pltpu.get_barrier_semaphore()

    def signal(sec, seq):
        pl.semaphore_signal(barrier, inc=1, device_id=(sec, seq), device_id_type=MESH)

    def device_of(j):
        return my_first * group_devs + j

    def each_group(body):
        for g in reversed(range(core_groups)):
            if g < few:
                body(g)
            else:
                pl.when(g < my_count)(functools.partial(body, g))

    def on_core(body):
        for c in range(2):
            pl.when(core == c)(functools.partial(body, c))

    def landed(region, sem):
        pltpu.make_async_copy(region, region, sem).wait()

    @pl.when(section > 0)
    def _():
        def greet(g):
            for j in range(g * group_devs, (g + 1) * group_devs):
                source = device_of(j)

                @pl.when(source != me)
                def _():
                    signal(section, source)

        each_group(greet)
        signal(section, sibling)

        @pl.when(span < last_span)
        def _():
            signal(section, me + 2)

        @pl.when(leads & (span < last_span))
        def _():
            signal(section, me + 4)

    @pl.when(section < last_section)
    def _():
        for z in range(spans):
            signal(section + 1, 2 * z + owner_core)

    own_tok = pl.ds(pl.multiple_of(core * tok, tok), tok)
    sib_tok = pl.ds(pl.multiple_of((1 - core) * tok, tok), tok)
    zero_copy = pltpu.make_async_copy(zeros, res_ref.at[0], zero_sem)

    @pl.when(section == last_section)
    def _():
        zeros[...] = jnp.zeros_like(zeros)
        zero_copy.start()

    @pl.when(section > 0)
    def _():
        small = [
            pltpu.make_async_copy(decay_hbm, decay_ref, small_sem.at[0]),
            pltpu.make_async_copy(skip_hbm, skip_ref, small_sem.at[1]),
            pltpu.make_async_copy(seg_hbm, seg_ref, small_sem.at[2]),
        ]
        own_steps = pltpu.make_async_copy(step_ref.at[0], all_steps.at[:, own_tok], own_sem.at[0])

        def own_copies(c):
            mine, kept_at = pl.ds(firsts[c], counts[c]), pl.ds(0, counts[c])
            return (
                pltpu.make_async_copy(out_proj_ref.at[0, mine], read.at[kept_at, own_tok, :], own_sem.at[1]),
                pltpu.make_async_copy(in_ref.at[0, mine], write.at[kept_at, own_tok, :], own_sem.at[2]),
            )

        @on_core
        def _(c):
            for copy in own_copies(c):
                copy.start()

        decay[...] = jnp.zeros_like(decay)
        for copy in small + [own_steps]:
            copy.start()
        to_self = (core == owner_core).astype(jnp.int32)
        after_first = (span > 0).astype(jnp.int32)
        hands_two = (leads & (span > 1)).astype(jnp.int32)
        pl.semaphore_wait(barrier, half - to_self + 1 + after_first + hands_two + my_count * group_devs)

        def pair_copies(c):
            theirs, kept_at = pl.ds(firsts[1 - c], counts[1 - c]), pl.ds(0, counts[1 - c])
            return [
                pltpu.make_async_remote_copy(
                    src_ref=src, dst_ref=dst, send_sem=pair_send.at[number], recv_sem=pair_recv.at[number],
                    device_id=(section, sibling), device_id_type=MESH,
                )
                for number, (src, dst) in enumerate((
                    (step_ref.at[0], all_steps.at[:, own_tok]),
                    (out_proj_ref.at[0, theirs], read.at[kept_at, own_tok, :]),
                    (in_ref.at[0, theirs], write.at[kept_at, own_tok, :]),
                ))
            ]

        @on_core
        def _(c):
            pair_copies(c)[0].start()

            @pl.when(span == last_span)
            def _():
                pair_copies(c)[1].start()

        for copy in small:
            copy.wait()
        for i in range(heads_dev):
            gains_send[i : i + 1, :] = jnp.full((1, LANES), decay_ref[0, i], F32)
            gains_send[heads_dev + i : heads_dev + i + 1, :] = jnp.full((1, LANES), skip_ref[0, i], F32)

        sends = []
        grad_slot = pl.ds(pl.multiple_of(slot * rows, rows), rows)
        for z in reversed(range(spans)):
            target = 2 * z + owner_core
            there = target != me
            piece = grad_ref.at[0, :, pl.ds(z * SPAN, SPAN)]
            grad_copy = pltpu.make_async_remote_copy(
                src_ref=piece, dst_ref=grad.at[grad_slot, :], send_sem=grad_send.at[z], recv_sem=grad_recv.at[slot],
                device_id=(section, target), device_id_type=MESH,
            )
            gain_copy = pltpu.make_async_remote_copy(
                src_ref=gains_send, dst_ref=gains.at[slot], send_sem=gain_send.at[z], recv_sem=gain_recv.at[slot],
                device_id=(section, target), device_id_type=MESH,
            )

            @pl.when(there)
            def _():
                gain_copy.start()
                grad_copy.start()

            @pl.when(jnp.logical_not(there))
            def _():
                pltpu.make_async_copy(gains_send, gains.at[slot], gain_recv.at[slot]).start()
                pltpu.make_async_copy(piece, grad.at[grad_slot, :], grad_recv.at[slot]).start()

            sends.append((there, grad_copy, gain_copy))

        @pl.when(span < last_span)
        def _():
            @on_core
            def _(c):
                pair_copies(c)[1].start()

        @on_core
        def _(c):
            pair_copies(c)[2].start()

        seg = seg_ref[0:1, pl.ds(base, SPAN)].astype(F32)
        before = pl.multiple_of(jnp.maximum(base - 128, 0), 128)
        prev_end = seg_ref[0:1, pl.ds(before, 128)].astype(F32)[:, 127:128]
        seg_end = seg[:, SPAN - 1 : SPAN]
        kept = (seg == prev_end).astype(F32)
        end_match = (seg == seg_end).astype(F32)
        joined = (seg_end == prev_end).astype(F32)
        t_index = lax.broadcasted_iota(jnp.int32, (SPAN, SPAN), 0)
        s_index = lax.broadcasted_iota(jnp.int32, (SPAN, SPAN), 1)
        summing = (t_index <= s_index).astype(F32)

        own_steps.wait()
        landed(all_steps.at[:, sib_tok], pair_recv.at[0])
        for g in range(core_groups):
            heads = all_steps[g * group_heads : (g + 1) * group_heads, :]
            if g < few:
                other = (core_groups + g) * group_heads
                heads = jnp.where(core == 0, all_steps[other : other + group_heads, :], heads)
            steps[g * group_heads : (g + 1) * group_heads, :] = heads
        step_rows = steps[...]
        running = jnp.dot(step_rows, summing, precision=lax.Precision.HIGHEST, preferred_element_type=F32)

        @each_group
        def _(g):
            for j in range(g * group_devs, (g + 1) * group_devs):
                landed(gains.at[j], gain_recv.at[j])
                decay[j * heads_dev : (j + 1) * heads_dev, :] = gains[j, 0:heads_dev, :]

        within = -decay[:, 0:1] * running
        grow = jnp.exp(within)
        shrink = step_rows * jnp.exp(-within)
        total = grow[:, SPAN - 1 : SPAN]
        factor = total * joined

        right_copies, above_copies, ahead_copies = [], [], []
        for g in range(core_groups):
            part = pl.ds(g * group_rows, group_rows)
            for copies, dst, send_sem, recv_sem, step in (
                (right_copies, right, right_send_sem, right_recv, 2),
                (above_copies, above, above_send, above_recv, 2),
                (ahead_copies, ahead, ahead_send, ahead_recv, 4),
            ):
                copies.append(pltpu.make_async_remote_copy(
                    src_ref=right_send.at[part, :], dst_ref=dst.at[part, :],
                    send_sem=send_sem.at[g], recv_sem=recv_sem.at[g],
                    device_id=(section, me - step), device_id_type=MESH,
                ))
        factor_copy = pltpu.make_async_remote_copy(
            src_ref=factor_send, dst_ref=above_factor, send_sem=factor_sem.at[0], recv_sem=factor_sem.at[1],
            device_id=(section, me - 2), device_id_type=MESH,
        )

        def hand_on(g):
            @pl.when(span > 1)
            def _():
                ahead_copies[g].start()

            @pl.when(span <= 1)
            def _():
                right_copies[g].start()

        @pl.when(follows & (span > 0))
        def _():
            factor_send[...] = jnp.broadcast_to(factor, factor_send.shape)
            factor_copy.start()

        @on_core
        def _(c):
            own_copies(c)[0].wait()
            landed(read.at[pl.ds(0, counts[c]), sib_tok, :], pair_recv.at[1])

        @each_group
        def _(g):
            for j in range(g * group_devs, (g + 1) * group_devs):
                landed(grad.at[pl.ds(j * rows, rows), :], grad_recv.at[j])
                for i in range(heads_dev):
                    head = j * heads_dev + i
                    part = pl.ds(head * width, width)
                    grown = grad[part, :].astype(F32) * grow[head : head + 1, :]
                    scaled[part, :] = grown.astype(BF16)
                    kept_scaled[part, :] = (grown * kept).astype(BF16)
            part = pl.ds(g * group_rows, group_rows)
            local_state[part, :] = dot_nn(kept_scaled[part, :], read[g])

            @pl.when(span == last_span)
            def _():
                right[part, :] = jnp.zeros((group_rows, right.shape[1]), BF16)
                if spans > 1:
                    right_send[part, :] = local_state[part, :].astype(BF16)
                    hand_on(g)

            @pl.when(follows & (span > 0))
            def _():
                right_send[part, :] = local_state[part, :].astype(BF16)
                above_copies[g].start()

        @pl.when((span == last_span) & (span > 1))
        def _():
            each_group(lambda g: right_copies[g].start())

        @on_core
        def _(c):
            own_copies(c)[1].wait()
            landed(write.at[pl.ds(0, counts[c]), sib_tok, :], pair_recv.at[2])

        seg_rows = jnp.broadcast_to(seg, (SPAN, SPAN))
        allowed = (t_index >= s_index) & (seg_rows == seg_rows.T)

        @each_group
        def _(g):
            part = pl.ds(g * group_rows, group_rows)
            masked = jnp.where(allowed, dot_nt(read[g], write[g]), 0.0).astype(BF16)
            inner[part, :] = dot_nn(scaled[part, :], masked)

        @pl.when(leads & (span < last_span))
        def _():
            landed(above_factor, factor_sem.at[1])

        @each_group
        def _(g):
            part = pl.ds(g * group_rows, group_rows)

            @pl.when(follows)
            def _():
                landed(right.at[part, :], right_recv.at[g])

            @pl.when(leads & (span < last_span))
            def _():
                landed(above.at[part, :], above_recv.at[g])
                landed(ahead.at[part, :], ahead_recv.at[g])
                for h in range(g * group_heads, (g + 1) * group_heads):
                    piece = pl.ds(h * width, width)
                    state = above[piece, :].astype(F32) + above_factor[h : h + 1, 0:1] * ahead[piece, :].astype(F32)
                    right[piece, :] = state.astype(BF16)
                    right_send[piece, :] = (local_state[piece, :] + factor[h : h + 1, :] * state).astype(BF16)

                @pl.when(span > 0)
                def _():
                    hand_on(g)

        @pl.when(leads & (span < last_span) & (span > 1))
        def _():
            each_group(lambda g: right_copies[g].start())

        def res_copy(j):
            return pltpu.make_async_remote_copy(
                src_ref=result.at[pl.ds(j * rows, rows), :], dst_ref=res_ref.at[0, :, pl.ds(base, SPAN)],
                send_sem=res_send.at[j], recv_sem=res_recv.at[span],
                device_id=(section - 1, device_of(j)), device_id_type=MESH,
            )

        @each_group
        def _(g):
            part = pl.ds(g * group_rows, group_rows)
            carried = dot_nt(right[part, :], write[g])
            for j in range(g * group_devs, (g + 1) * group_devs):
                for i in range(heads_dev):
                    head = j * heads_dev + i
                    piece = pl.ds(head * width, width)
                    first = (head - g * group_heads) * width
                    reach = end_match * total[head : head + 1, :]
                    result[piece, :] = (
                        shrink[head : head + 1, :] * (inner[piece, :] + reach * carried[first : first + width, :])
                        + gains[j, heads_dev + i : heads_dev + i + 1, 0:1] * grad[piece, :].astype(F32)
                    ).astype(BF16)
                res_copy(j).start()

        for there, grad_copy, gain_copy in sends:
            @pl.when(there)
            def _():
                grad_copy.wait_send()
                gain_copy.wait_send()

        @on_core
        def _(c):
            for copy in pair_copies(c):
                copy.wait_send()

        @pl.when(follows & (span > 0))
        def _():
            factor_copy.wait_send()

        @each_group
        def _(g):
            @pl.when(leads & (span > 0))
            def _():
                right_copies[g].wait_send()

            @pl.when(leads & (span > 1))
            def _():
                ahead_copies[g].wait_send()

            @pl.when(follows & (span > 0))
            def _():
                above_copies[g].wait_send()

            for j in range(g * group_devs, (g + 1) * group_devs):
                res_copy(j).wait_send()

    @pl.when(section < last_section)
    def _():
        for z in range(spans):
            landed(res_ref.at[0, :, pl.ds(z * SPAN, SPAN)], res_recv.at[z])

    @pl.when(section == last_section)
    def _():
        zero_copy.wait()


def solution(mesh):
    sections, devs = mesh.shape["section"], mesh.shape["seq"]
    placed = (
        P("section", "seq", None),
        P("section", None, "seq"),
        P("section", "seq"),
        P("section", "seq"),
        P("section", None, "seq", None),
        P("section", None, "seq", None),
        P("section", None),
    )

    def local(grad_out, step_sizes, decay_rate, skip_gain, state_in, state_out, segment_ids):
        rows, seqlen = grad_out.shape[1:]
        heads_dev = decay_rate.shape[1]
        groups, _, state = state_in.shape[1:]
        half = devs // 2
        core_groups = group_counts(groups)[1]
        slots = core_groups * (devs // groups)
        all_rows = slots * rows
        core_heads = slots * heads_dev
        gain_rows = -(-2 * heads_dev // 8) * 8
        dma = pltpu.SemaphoreType.DMA
        anywhere = pl.BlockSpec(memory_space=pl.ANY)
        return pl.pallas_call(
            functools.partial(kernel, sections, devs),
            out_shape=pltpu.VMEM(grad_out.shape, BF16),
            in_specs=[anywhere] * 7,
            out_specs=anywhere,
            scratch_shapes=[
                pltpu.SMEM(decay_rate.shape, F32),
                pltpu.SMEM(skip_gain.shape, F32),
                pltpu.VMEM(segment_ids.shape, jnp.int32),
                pltpu.VMEM((gain_rows, LANES), F32),
                pltpu.VMEM((slots, gain_rows, LANES), F32),
                pltpu.VMEM((core_heads, LANES), F32),
                pltpu.VMEM((step_sizes.shape[1], SPAN), F32),
                pltpu.VMEM((core_heads, SPAN), F32),
                pltpu.VMEM((core_groups, SPAN, state), BF16),
                pltpu.VMEM((core_groups, SPAN, state), BF16),
                pltpu.VMEM((all_rows, SPAN), BF16),
                pltpu.VMEM((all_rows, SPAN), BF16),
                pltpu.VMEM((all_rows, SPAN), BF16),
                pltpu.VMEM((all_rows, SPAN), F32),
                pltpu.VMEM((all_rows, state), F32),
                pltpu.VMEM((all_rows, state), BF16),
                pltpu.VMEM((all_rows, state), BF16),
                pltpu.VMEM((all_rows, state), BF16),
                pltpu.VMEM((all_rows, state), BF16),
                pltpu.VMEM((core_heads, LANES), F32),
                pltpu.VMEM((core_heads, LANES), F32),
                pltpu.VMEM((all_rows, SPAN), BF16),
                pltpu.VMEM((rows, seqlen), BF16),
                dma((half,)), dma((slots,)), dma((half,)), dma((slots,)),
                dma((3,)), dma((3,)), dma((3,)),
                dma((core_groups,)), dma((core_groups,)), dma((core_groups,)),
                dma((core_groups,)), dma((core_groups,)), dma((core_groups,)), dma((2,)),
                dma((slots,)), dma((half,)), dma, dma((3,)),
            ],
            compiler_params=pltpu.CompilerParams(
                collective_id=0, has_side_effects=True, vmem_limit_bytes=64 * MIB - MIB * 3 // 4 - 2 * rows * seqlen
            ),
        )(
            grad_out, step_sizes, decay_rate, skip_gain,
            state_in, state_out, segment_ids,
        )

    return jax.shard_map(
        local, mesh=mesh, in_specs=placed, out_specs=P("section", "seq", None), check_vma=False
    )
```

```python
import functools

import jax
import jax.numpy as jnp
from jax import lax
from jax.experimental import pallas as pl
from jax.experimental.pallas import tpu as pltpu
from jax.sharding import PartitionSpec as P

SPAN = 256
LANES = 128
MIB = 1024 * 1024


def group_counts(groups):
    few = 3 * groups // 8
    return few, groups - few
MESH = pl.DeviceIdType.MESH
F32, BF16 = jnp.float32, jnp.bfloat16


def dot_nt(a, b):
    return lax.dot_general(a, b, (((1,), (1,)), ((), ())), preferred_element_type=F32)


def dot_nn(a, b):
    return jnp.dot(a, b, preferred_element_type=F32)


def kernel(
    sections, devs,
    grad_ref, step_ref, decay_hbm, skip_hbm, in_ref, out_proj_ref, seg_hbm,
    res_ref,
    decay_ref, skip_ref, seg_ref, gains_send, gains, decay, all_steps, steps, write, read, grad, scaled, kept_scaled, inner, local_state,
    right, right_send, above, ahead, factor_send, above_factor, result, zeros,
    grad_send, grad_recv, gain_send, gain_recv, pair_send, pair_recv, own_sem, right_send_sem, right_recv,
    above_send, above_recv, ahead_send, ahead_recv, factor_sem,
    res_send, res_recv, zero_sem, small_sem,
):
    half = devs // 2
    spans = devs // 2
    rows, heads_dev = grad_ref.shape[1], decay_hbm.shape[1]
    width = rows // heads_dev
    tok = step_ref.shape[2]
    groups = in_ref.shape[1]
    counts = few, core_groups = group_counts(groups)
    firsts = core_groups, 0
    group_devs = devs // groups
    group_rows = group_devs * rows
    group_heads = group_devs * heads_dev

    section = lax.axis_index("section")
    me = lax.axis_index("seq")
    span = me // 2
    core = me % 2
    sibling = 2 * span + 1 - core
    own_group = me // group_devs
    owner_core = (own_group < core_groups).astype(jnp.int32)
    slot = me - (1 - owner_core) * core_groups * group_devs
    my_first = (1 - core) * core_groups
    my_count = few + core * (core_groups - few)
    base = pl.multiple_of(span * SPAN, SPAN)
    last_section = sections - 1
    last_span = spans - 1
    leads = (last_span - span) % 2 == 0
    follows = jnp.logical_not(leads)
    barrier = pltpu.get_barrier_semaphore()

    def signal(sec, seq):
        pl.semaphore_signal(barrier, inc=1, device_id=(sec, seq), device_id_type=MESH)

    def device_of(j):
        return my_first * group_devs + j

    def each_group(body):
        for g in reversed(range(core_groups)):
            if g < few:
                body(g)
            else:
                pl.when(g < my_count)(functools.partial(body, g))

    def on_core(body):
        for c in range(2):
            pl.when(core == c)(functools.partial(body, c))

    def landed(region, sem):
        pltpu.make_async_copy(region, region, sem).wait()

    @pl.when(section > 0)
    def _():
        def greet(g):
            for j in range(g * group_devs, (g + 1) * group_devs):
                source = device_of(j)

                @pl.when(source != me)
                def _():
                    signal(section, source)

        each_group(greet)
        signal(section, sibling)

        @pl.when(span < last_span)
        def _():
            signal(section, me + 2)

        @pl.when(leads & (span < last_span))
        def _():
            signal(section, me + 4)

    @pl.when(section < last_section)
    def _():
        for z in range(spans):
            signal(section + 1, 2 * z + owner_core)

    own_tok = pl.ds(pl.multiple_of(core * tok, tok), tok)
    sib_tok = pl.ds(pl.multiple_of((1 - core) * tok, tok), tok)
    zero_copy = pltpu.make_async_copy(zeros, res_ref.at[0], zero_sem)

    @pl.when(section == last_section)
    def _():
        zeros[...] = jnp.zeros_like(zeros)
        zero_copy.start()

    @pl.when(section > 0)
    def _():
        small = [
            pltpu.make_async_copy(decay_hbm, decay_ref, small_sem.at[0]),
            pltpu.make_async_copy(skip_hbm, skip_ref, small_sem.at[1]),
            pltpu.make_async_copy(seg_hbm, seg_ref, small_sem.at[2]),
        ]
        own_steps = pltpu.make_async_copy(step_ref.at[0], all_steps.at[:, own_tok], own_sem.at[0])

        def own_copies(c):
            mine, kept_at = pl.ds(firsts[c], counts[c]), pl.ds(0, counts[c])
            return (
                pltpu.make_async_copy(out_proj_ref.at[0, mine], read.at[kept_at, own_tok, :], own_sem.at[1]),
                pltpu.make_async_copy(in_ref.at[0, mine], write.at[kept_at, own_tok, :], own_sem.at[2]),
            )

        @on_core
        def _(c):
            for copy in own_copies(c):
                copy.start()

        decay[...] = jnp.zeros_like(decay)
        for copy in small + [own_steps]:
            copy.start()
        to_self = (core == owner_core).astype(jnp.int32)
        after_first = (span > 0).astype(jnp.int32)
        hands_two = (leads & (span > 1)).astype(jnp.int32)
        pl.semaphore_wait(barrier, half - to_self + 1 + after_first + hands_two + my_count * group_devs)

        def pair_copies(c):
            theirs, kept_at = pl.ds(firsts[1 - c], counts[1 - c]), pl.ds(0, counts[1 - c])
            return [
                pltpu.make_async_remote_copy(
                    src_ref=src, dst_ref=dst, send_sem=pair_send.at[number], recv_sem=pair_recv.at[number],
                    device_id=(section, sibling), device_id_type=MESH,
                )
                for number, (src, dst) in enumerate((
                    (step_ref.at[0], all_steps.at[:, own_tok]),
                    (out_proj_ref.at[0, theirs], read.at[kept_at, own_tok, :]),
                    (in_ref.at[0, theirs], write.at[kept_at, own_tok, :]),
                ))
            ]

        @on_core
        def _(c):
            pair_copies(c)[0].start()

            @pl.when(span == last_span)
            def _():
                pair_copies(c)[1].start()

        for copy in small:
            copy.wait()
        for i in range(heads_dev):
            gains_send[i : i + 1, :] = jnp.full((1, LANES), decay_ref[0, i], F32)
            gains_send[heads_dev + i : heads_dev + i + 1, :] = jnp.full((1, LANES), skip_ref[0, i], F32)

        sends = []
        grad_slot = pl.ds(pl.multiple_of(slot * rows, rows), rows)
        for z in reversed(range(spans)):
            target = 2 * z + owner_core
            there = target != me
            piece = grad_ref.at[0, :, pl.ds(z * SPAN, SPAN)]
            grad_copy = pltpu.make_async_remote_copy(
                src_ref=piece, dst_ref=grad.at[grad_slot, :], send_sem=grad_send.at[z], recv_sem=grad_recv.at[slot],
                device_id=(section, target), device_id_type=MESH,
            )
            gain_copy = pltpu.make_async_remote_copy(
                src_ref=gains_send, dst_ref=gains.at[slot], send_sem=gain_send.at[z], recv_sem=gain_recv.at[slot],
                device_id=(section, target), device_id_type=MESH,
            )

            @pl.when(there)
            def _():
                gain_copy.start()
                grad_copy.start()

            @pl.when(jnp.logical_not(there))
            def _():
                pltpu.make_async_copy(gains_send, gains.at[slot], gain_recv.at[slot]).start()
                pltpu.make_async_copy(piece, grad.at[grad_slot, :], grad_recv.at[slot]).start()

            sends.append((there, grad_copy, gain_copy))

        @pl.when(span < last_span)
        def _():
            @on_core
            def _(c):
                pair_copies(c)[1].start()

        @on_core
        def _(c):
            pair_copies(c)[2].start()

        seg = seg_ref[0:1, pl.ds(base, SPAN)].astype(F32)
        before = pl.multiple_of(jnp.maximum(base - 128, 0), 128)
        prev_end = seg_ref[0:1, pl.ds(before, 128)].astype(F32)[:, 127:128]
        seg_end = seg[:, SPAN - 1 : SPAN]
        kept = (seg == prev_end).astype(F32)
        end_match = (seg == seg_end).astype(F32)
        joined = (seg_end == prev_end).astype(F32)
        t_index = lax.broadcasted_iota(jnp.int32, (SPAN, SPAN), 0)
        s_index = lax.broadcasted_iota(jnp.int32, (SPAN, SPAN), 1)
        summing = (t_index <= s_index).astype(F32)

        own_steps.wait()
        landed(all_steps.at[:, sib_tok], pair_recv.at[0])
        for g in range(core_groups):
            heads = all_steps[g * group_heads : (g + 1) * group_heads, :]
            if g < few:
                other = (core_groups + g) * group_heads
                heads = jnp.where(core == 0, all_steps[other : other + group_heads, :], heads)
            steps[g * group_heads : (g + 1) * group_heads, :] = heads
        step_rows = steps[...]
        running = jnp.dot(step_rows, summing, precision=lax.Precision.HIGHEST, preferred_element_type=F32)

        @each_group
        def _(g):
            for j in range(g * group_devs, (g + 1) * group_devs):
                landed(gains.at[j], gain_recv.at[j])
                decay[j * heads_dev : (j + 1) * heads_dev, :] = gains[j, 0:heads_dev, :]

        within = -decay[:, 0:1] * running
        grow = jnp.exp(within)
        shrink = step_rows * jnp.exp(-within)
        total = grow[:, SPAN - 1 : SPAN]
        factor = total * joined

        right_copies, above_copies, ahead_copies = [], [], []
        for g in range(core_groups):
            part = pl.ds(g * group_rows, group_rows)
            for copies, dst, send_sem, recv_sem, step in (
                (right_copies, right, right_send_sem, right_recv, 2),
                (above_copies, above, above_send, above_recv, 2),
                (ahead_copies, ahead, ahead_send, ahead_recv, 4),
            ):
                copies.append(pltpu.make_async_remote_copy(
                    src_ref=right_send.at[part, :], dst_ref=dst.at[part, :],
                    send_sem=send_sem.at[g], recv_sem=recv_sem.at[g],
                    device_id=(section, me - step), device_id_type=MESH,
                ))
        factor_copy = pltpu.make_async_remote_copy(
            src_ref=factor_send, dst_ref=above_factor, send_sem=factor_sem.at[0], recv_sem=factor_sem.at[1],
            device_id=(section, me - 2), device_id_type=MESH,
        )

        def hand_on(g):
            @pl.when(span > 1)
            def _():
                ahead_copies[g].start()

            @pl.when(span <= 1)
            def _():
                right_copies[g].start()

        @pl.when(follows & (span > 0))
        def _():
            factor_send[...] = jnp.broadcast_to(factor, factor_send.shape)
            factor_copy.start()

        @on_core
        def _(c):
            own_copies(c)[0].wait()
            landed(read.at[pl.ds(0, counts[c]), sib_tok, :], pair_recv.at[1])

        @each_group
        def _(g):
            for j in range(g * group_devs, (g + 1) * group_devs):
                landed(grad.at[pl.ds(j * rows, rows), :], grad_recv.at[j])
                for i in range(heads_dev):
                    head = j * heads_dev + i
                    part = pl.ds(head * width, width)
                    grown = grad[part, :].astype(F32) * grow[head : head + 1, :]
                    scaled[part, :] = grown.astype(BF16)
                    kept_scaled[part, :] = (grown * kept).astype(BF16)
            part = pl.ds(g * group_rows, group_rows)
            local_state[part, :] = dot_nn(kept_scaled[part, :], read[g])

            @pl.when(span == last_span)
            def _():
                right[part, :] = jnp.zeros((group_rows, right.shape[1]), BF16)
                if spans > 1:
                    right_send[part, :] = local_state[part, :].astype(BF16)
                    hand_on(g)

            @pl.when(follows & (span > 0))
            def _():
                right_send[part, :] = local_state[part, :].astype(BF16)
                above_copies[g].start()

        @pl.when((span == last_span) & (span > 1))
        def _():
            each_group(lambda g: right_copies[g].start())

        @on_core
        def _(c):
            own_copies(c)[1].wait()
            landed(write.at[pl.ds(0, counts[c]), sib_tok, :], pair_recv.at[2])

        seg_rows = jnp.broadcast_to(seg, (SPAN, SPAN))
        allowed = (t_index >= s_index) & (seg_rows == seg_rows.T)

        @each_group
        def _(g):
            part = pl.ds(g * group_rows, group_rows)
            masked = jnp.where(allowed, dot_nt(read[g], write[g]), 0.0).astype(BF16)
            inner[part, :] = dot_nn(scaled[part, :], masked)

        @pl.when(leads & (span < last_span))
        def _():
            landed(above_factor, factor_sem.at[1])

        @each_group
        def _(g):
            part = pl.ds(g * group_rows, group_rows)

            @pl.when(leads & (span < last_span))
            def _():
                landed(above.at[part, :], above_recv.at[g])
                landed(ahead.at[part, :], ahead_recv.at[g])
                for h in range(g * group_heads, (g + 1) * group_heads):
                    piece = pl.ds(h * width, width)
                    state = above[piece, :].astype(F32) + above_factor[h : h + 1, 0:1] * ahead[piece, :].astype(F32)
                    right[piece, :] = state.astype(BF16)
                    right_send[piece, :] = (local_state[piece, :] + factor[h : h + 1, :] * state).astype(BF16)

                @pl.when(span > 0)
                def _():
                    hand_on(g)

        @pl.when(leads & (span < last_span) & (span > 1))
        def _():
            each_group(lambda g: right_copies[g].start())

        def res_copy(j):
            return pltpu.make_async_remote_copy(
                src_ref=result.at[pl.ds(j * rows, rows), :], dst_ref=res_ref.at[0, :, pl.ds(base, SPAN)],
                send_sem=res_send.at[j], recv_sem=res_recv.at[span],
                device_id=(section - 1, device_of(j)), device_id_type=MESH,
            )

        @each_group
        def _(g):
            part = pl.ds(g * group_rows, group_rows)

            @pl.when(follows)
            def _():
                landed(right.at[part, :], right_recv.at[g])

            carried = dot_nt(right[part, :], write[g])
            for j in range(g * group_devs, (g + 1) * group_devs):
                for i in range(heads_dev):
                    head = j * heads_dev + i
                    piece = pl.ds(head * width, width)
                    first = (head - g * group_heads) * width
                    reach = end_match * total[head : head + 1, :]
                    result[piece, :] = (
                        shrink[head : head + 1, :] * (inner[piece, :] + reach * carried[first : first + width, :])
                        + gains[j, heads_dev + i : heads_dev + i + 1, 0:1] * grad[piece, :].astype(F32)
                    ).astype(BF16)
                res_copy(j).start()

        for there, grad_copy, gain_copy in sends:
            @pl.when(there)
            def _():
                grad_copy.wait_send()
                gain_copy.wait_send()

        @on_core
        def _(c):
            for copy in pair_copies(c):
                copy.wait_send()

        @pl.when(follows & (span > 0))
        def _():
            factor_copy.wait_send()

        @each_group
        def _(g):
            @pl.when(leads & (span > 0))
            def _():
                right_copies[g].wait_send()

            @pl.when(leads & (span > 1))
            def _():
                ahead_copies[g].wait_send()

            @pl.when(follows & (span > 0))
            def _():
                above_copies[g].wait_send()

            for j in range(g * group_devs, (g + 1) * group_devs):
                res_copy(j).wait_send()

    @pl.when(section < last_section)
    def _():
        for z in range(spans):
            landed(res_ref.at[0, :, pl.ds(z * SPAN, SPAN)], res_recv.at[z])

    @pl.when(section == last_section)
    def _():
        zero_copy.wait()


def solution(mesh):
    sections, devs = mesh.shape["section"], mesh.shape["seq"]
    placed = (
        P("section", "seq", None),
        P("section", None, "seq"),
        P("section", "seq"),
        P("section", "seq"),
        P("section", None, "seq", None),
        P("section", None, "seq", None),
        P("section", None),
    )

    def local(grad_out, step_sizes, decay_rate, skip_gain, state_in, state_out, segment_ids):
        rows, seqlen = grad_out.shape[1:]
        heads_dev = decay_rate.shape[1]
        groups, _, state = state_in.shape[1:]
        half = devs // 2
        core_groups = group_counts(groups)[1]
        slots = core_groups * (devs // groups)
        all_rows = slots * rows
        core_heads = slots * heads_dev
        gain_rows = -(-2 * heads_dev // 8) * 8
        dma = pltpu.SemaphoreType.DMA
        anywhere = pl.BlockSpec(memory_space=pl.ANY)
        return pl.pallas_call(
            functools.partial(kernel, sections, devs),
            out_shape=pltpu.VMEM(grad_out.shape, BF16),
            in_specs=[anywhere] * 7,
            out_specs=anywhere,
            scratch_shapes=[
                pltpu.SMEM(decay_rate.shape, F32),
                pltpu.SMEM(skip_gain.shape, F32),
                pltpu.VMEM(segment_ids.shape, jnp.int32),
                pltpu.VMEM((gain_rows, LANES), F32),
                pltpu.VMEM((slots, gain_rows, LANES), F32),
                pltpu.VMEM((core_heads, LANES), F32),
                pltpu.VMEM((step_sizes.shape[1], SPAN), F32),
                pltpu.VMEM((core_heads, SPAN), F32),
                pltpu.VMEM((core_groups, SPAN, state), BF16),
                pltpu.VMEM((core_groups, SPAN, state), BF16),
                pltpu.VMEM((all_rows, SPAN), BF16),
                pltpu.VMEM((all_rows, SPAN), BF16),
                pltpu.VMEM((all_rows, SPAN), BF16),
                pltpu.VMEM((all_rows, SPAN), F32),
                pltpu.VMEM((all_rows, state), F32),
                pltpu.VMEM((all_rows, state), BF16),
                pltpu.VMEM((all_rows, state), BF16),
                pltpu.VMEM((all_rows, state), BF16),
                pltpu.VMEM((all_rows, state), BF16),
                pltpu.VMEM((core_heads, LANES), F32),
                pltpu.VMEM((core_heads, LANES), F32),
                pltpu.VMEM((all_rows, SPAN), BF16),
                pltpu.VMEM((rows, seqlen), BF16),
                dma((half,)), dma((slots,)), dma((half,)), dma((slots,)),
                dma((3,)), dma((3,)), dma((3,)),
                dma((core_groups,)), dma((core_groups,)), dma((core_groups,)),
                dma((core_groups,)), dma((core_groups,)), dma((core_groups,)), dma((2,)),
                dma((slots,)), dma((half,)), dma, dma((3,)),
            ],
            compiler_params=pltpu.CompilerParams(
                collective_id=0, has_side_effects=True, vmem_limit_bytes=64 * MIB - MIB * 3 // 4 - 2 * rows * seqlen
            ),
        )(
            grad_out, step_sizes, decay_rate, skip_gain,
            state_in, state_out, segment_ids,
        )

    return jax.shard_map(
        local, mesh=mesh, in_specs=placed, out_specs=P("section", "seq", None), check_vma=False
    )
```

```python
import functools

import jax
import jax.numpy as jnp
from jax import lax
from jax.experimental import pallas as pl
from jax.experimental.pallas import tpu as pltpu
from jax.sharding import PartitionSpec as P

SPAN = 256
LANES = 128
MIB = 1024 * 1024


def group_counts(groups):
    few = groups // 4
    return few, groups - few
MESH = pl.DeviceIdType.MESH
F32, BF16 = jnp.float32, jnp.bfloat16


def dot_nt(a, b):
    return lax.dot_general(a, b, (((1,), (1,)), ((), ())), preferred_element_type=F32)


def dot_nn(a, b):
    return jnp.dot(a, b, preferred_element_type=F32)


def kernel(
    sections, devs,
    grad_ref, step_ref, decay_hbm, skip_hbm, in_ref, out_proj_ref, seg_hbm,
    res_ref,
    decay_ref, skip_ref, seg_ref, gains_send, gains, decay, all_steps, steps, write, read, grad, scaled, kept_scaled, inner, local_state,
    right, right_send, above, ahead, factor_send, above_factor, result, zeros,
    grad_send, grad_recv, gain_send, gain_recv, pair_send, pair_recv, own_sem, right_send_sem, right_recv,
    above_send, above_recv, ahead_send, ahead_recv, factor_sem,
    res_send, res_recv, zero_sem, small_sem,
):
    half = devs // 2
    spans = devs // 2
    rows, heads_dev = grad_ref.shape[1], decay_hbm.shape[1]
    width = rows // heads_dev
    tok = step_ref.shape[2]
    groups = in_ref.shape[1]
    counts = few, core_groups = group_counts(groups)
    firsts = core_groups, 0
    group_devs = devs // groups
    group_rows = group_devs * rows
    group_heads = group_devs * heads_dev

    section = lax.axis_index("section")
    me = lax.axis_index("seq")
    span = me // 2
    core = me % 2
    sibling = 2 * span + 1 - core
    own_group = me // group_devs
    owner_core = (own_group < core_groups).astype(jnp.int32)
    slot = me - (1 - owner_core) * core_groups * group_devs
    my_first = (1 - core) * core_groups
    my_count = few + core * (core_groups - few)
    base = pl.multiple_of(span * SPAN, SPAN)
    last_section = sections - 1
    last_span = spans - 1
    leads = (last_span - span) % 2 == 0
    follows = jnp.logical_not(leads)
    barrier = pltpu.get_barrier_semaphore()

    def signal(sec, seq):
        pl.semaphore_signal(barrier, inc=1, device_id=(sec, seq), device_id_type=MESH)

    def device_of(j):
        return my_first * group_devs + j

    def each_group(body):
        for g in reversed(range(core_groups)):
            if g < few:
                body(g)
            else:
                pl.when(g < my_count)(functools.partial(body, g))

    def on_core(body):
        for c in range(2):
            pl.when(core == c)(functools.partial(body, c))

    def landed(region, sem):
        pltpu.make_async_copy(region, region, sem).wait()

    @pl.when(section > 0)
    def _():
        def greet(g):
            for j in range(g * group_devs, (g + 1) * group_devs):
                source = device_of(j)

                @pl.when(source != me)
                def _():
                    signal(section, source)

        each_group(greet)
        signal(section, sibling)

        @pl.when(span < last_span)
        def _():
            signal(section, me + 2)

        @pl.when(leads & (span < last_span))
        def _():
            signal(section, me + 4)

    @pl.when(section < last_section)
    def _():
        for z in range(spans):
            signal(section + 1, 2 * z + owner_core)

    own_tok = pl.ds(pl.multiple_of(core * tok, tok), tok)
    sib_tok = pl.ds(pl.multiple_of((1 - core) * tok, tok), tok)
    zero_copy = pltpu.make_async_copy(zeros, res_ref.at[0], zero_sem)

    @pl.when(section == last_section)
    def _():
        zeros[...] = jnp.zeros_like(zeros)
        zero_copy.start()

    @pl.when(section > 0)
    def _():
        small = [
            pltpu.make_async_copy(decay_hbm, decay_ref, small_sem.at[0]),
            pltpu.make_async_copy(skip_hbm, skip_ref, small_sem.at[1]),
            pltpu.make_async_copy(seg_hbm, seg_ref, small_sem.at[2]),
        ]
        own_steps = pltpu.make_async_copy(step_ref.at[0], all_steps.at[:, own_tok], own_sem.at[0])

        def own_copies(c):
            mine, kept_at = pl.ds(firsts[c], counts[c]), pl.ds(0, counts[c])
            return (
                pltpu.make_async_copy(out_proj_ref.at[0, mine], read.at[kept_at, own_tok, :], own_sem.at[1]),
                pltpu.make_async_copy(in_ref.at[0, mine], write.at[kept_at, own_tok, :], own_sem.at[2]),
            )

        @on_core
        def _(c):
            for copy in own_copies(c):
                copy.start()

        decay[...] = jnp.zeros_like(decay)
        for copy in small + [own_steps]:
            copy.start()
        to_self = (core == owner_core).astype(jnp.int32)
        after_first = (span > 0).astype(jnp.int32)
        hands_two = (leads & (span > 1)).astype(jnp.int32)
        pl.semaphore_wait(barrier, half - to_self + 1 + after_first + hands_two + my_count * group_devs)

        def pair_copies(c):
            theirs, kept_at = pl.ds(firsts[1 - c], counts[1 - c]), pl.ds(0, counts[1 - c])
            return [
                pltpu.make_async_remote_copy(
                    src_ref=src, dst_ref=dst, send_sem=pair_send.at[number], recv_sem=pair_recv.at[number],
                    device_id=(section, sibling), device_id_type=MESH,
                )
                for number, (src, dst) in enumerate((
                    (step_ref.at[0], all_steps.at[:, own_tok]),
                    (out_proj_ref.at[0, theirs], read.at[kept_at, own_tok, :]),
                    (in_ref.at[0, theirs], write.at[kept_at, own_tok, :]),
                ))
            ]

        @on_core
        def _(c):
            pair_copies(c)[0].start()

            @pl.when(span == last_span)
            def _():
                pair_copies(c)[1].start()

        for copy in small:
            copy.wait()
        for i in range(heads_dev):
            gains_send[i : i + 1, :] = jnp.full((1, LANES), decay_ref[0, i], F32)
            gains_send[heads_dev + i : heads_dev + i + 1, :] = jnp.full((1, LANES), skip_ref[0, i], F32)

        sends = []
        grad_slot = pl.ds(pl.multiple_of(slot * rows, rows), rows)
        for z in reversed(range(spans)):
            target = 2 * z + owner_core
            there = target != me
            piece = grad_ref.at[0, :, pl.ds(z * SPAN, SPAN)]
            grad_copy = pltpu.make_async_remote_copy(
                src_ref=piece, dst_ref=grad.at[grad_slot, :], send_sem=grad_send.at[z], recv_sem=grad_recv.at[slot],
                device_id=(section, target), device_id_type=MESH,
            )
            gain_copy = pltpu.make_async_remote_copy(
                src_ref=gains_send, dst_ref=gains.at[slot], send_sem=gain_send.at[z], recv_sem=gain_recv.at[slot],
                device_id=(section, target), device_id_type=MESH,
            )

            @pl.when(there)
            def _():
                gain_copy.start()
                grad_copy.start()

            @pl.when(jnp.logical_not(there))
            def _():
                pltpu.make_async_copy(gains_send, gains.at[slot], gain_recv.at[slot]).start()
                pltpu.make_async_copy(piece, grad.at[grad_slot, :], grad_recv.at[slot]).start()

            sends.append((there, grad_copy, gain_copy))

        @pl.when(span < last_span)
        def _():
            @on_core
            def _(c):
                pair_copies(c)[1].start()

        @on_core
        def _(c):
            pair_copies(c)[2].start()

        seg = seg_ref[0:1, pl.ds(base, SPAN)].astype(F32)
        before = pl.multiple_of(jnp.maximum(base - 128, 0), 128)
        prev_end = seg_ref[0:1, pl.ds(before, 128)].astype(F32)[:, 127:128]
        seg_end = seg[:, SPAN - 1 : SPAN]
        kept = (seg == prev_end).astype(F32)
        end_match = (seg == seg_end).astype(F32)
        joined = (seg_end == prev_end).astype(F32)
        t_index = lax.broadcasted_iota(jnp.int32, (SPAN, SPAN), 0)
        s_index = lax.broadcasted_iota(jnp.int32, (SPAN, SPAN), 1)
        summing = (t_index <= s_index).astype(F32)

        own_steps.wait()
        landed(all_steps.at[:, sib_tok], pair_recv.at[0])
        for g in range(core_groups):
            heads = all_steps[g * group_heads : (g + 1) * group_heads, :]
            if g < few:
                other = (core_groups + g) * group_heads
                heads = jnp.where(core == 0, all_steps[other : other + group_heads, :], heads)
            steps[g * group_heads : (g + 1) * group_heads, :] = heads
        step_rows = steps[...]
        running = jnp.dot(step_rows, summing, precision=lax.Precision.HIGHEST, preferred_element_type=F32)

        @each_group
        def _(g):
            for j in range(g * group_devs, (g + 1) * group_devs):
                landed(gains.at[j], gain_recv.at[j])
                decay[j * heads_dev : (j + 1) * heads_dev, :] = gains[j, 0:heads_dev, :]

        within = -decay[:, 0:1] * running
        grow = jnp.exp(within)
        shrink = step_rows * jnp.exp(-within)
        total = grow[:, SPAN - 1 : SPAN]
        factor = total * joined

        right_copies, above_copies, ahead_copies = [], [], []
        for g in range(core_groups):
            part = pl.ds(g * group_rows, group_rows)
            for copies, dst, send_sem, recv_sem, step in (
                (right_copies, right, right_send_sem, right_recv, 2),
                (above_copies, above, above_send, above_recv, 2),
                (ahead_copies, ahead, ahead_send, ahead_recv, 4),
            ):
                copies.append(pltpu.make_async_remote_copy(
                    src_ref=right_send.at[part, :], dst_ref=dst.at[part, :],
                    send_sem=send_sem.at[g], recv_sem=recv_sem.at[g],
                    device_id=(section, me - step), device_id_type=MESH,
                ))
        factor_copy = pltpu.make_async_remote_copy(
            src_ref=factor_send, dst_ref=above_factor, send_sem=factor_sem.at[0], recv_sem=factor_sem.at[1],
            device_id=(section, me - 2), device_id_type=MESH,
        )

        def hand_on(g):
            @pl.when(span > 1)
            def _():
                ahead_copies[g].start()

            @pl.when(span <= 1)
            def _():
                right_copies[g].start()

        @pl.when(follows & (span > 0))
        def _():
            factor_send[...] = jnp.broadcast_to(factor, factor_send.shape)
            factor_copy.start()

        @on_core
        def _(c):
            own_copies(c)[0].wait()
            landed(read.at[pl.ds(0, counts[c]), sib_tok, :], pair_recv.at[1])

        @each_group
        def _(g):
            for j in range(g * group_devs, (g + 1) * group_devs):
                landed(grad.at[pl.ds(j * rows, rows), :], grad_recv.at[j])
                for i in range(heads_dev):
                    head = j * heads_dev + i
                    part = pl.ds(head * width, width)
                    grown = grad[part, :].astype(F32) * grow[head : head + 1, :]
                    scaled[part, :] = grown.astype(BF16)
                    kept_scaled[part, :] = (grown * kept).astype(BF16)
            part = pl.ds(g * group_rows, group_rows)
            local_state[part, :] = dot_nn(kept_scaled[part, :], read[g])

            @pl.when(span == last_span)
            def _():
                right[part, :] = jnp.zeros((group_rows, right.shape[1]), BF16)
                if spans > 1:
                    right_send[part, :] = local_state[part, :].astype(BF16)
                    hand_on(g)

            @pl.when(follows & (span > 0))
            def _():
                right_send[part, :] = local_state[part, :].astype(BF16)
                above_copies[g].start()

        @pl.when((span == last_span) & (span > 1))
        def _():
            each_group(lambda g: right_copies[g].start())

        @on_core
        def _(c):
            own_copies(c)[1].wait()
            landed(write.at[pl.ds(0, counts[c]), sib_tok, :], pair_recv.at[2])

        seg_rows = jnp.broadcast_to(seg, (SPAN, SPAN))
        allowed = (t_index >= s_index) & (seg_rows == seg_rows.T)

        @each_group
        def _(g):
            part = pl.ds(g * group_rows, group_rows)
            masked = jnp.where(allowed, dot_nt(read[g], write[g]), 0.0).astype(BF16)
            inner[part, :] = dot_nn(scaled[part, :], masked)

        @pl.when(leads & (span < last_span))
        def _():
            landed(above_factor, factor_sem.at[1])

        @each_group
        def _(g):
            part = pl.ds(g * group_rows, group_rows)

            @pl.when(leads & (span < last_span))
            def _():
                landed(above.at[part, :], above_recv.at[g])
                landed(ahead.at[part, :], ahead_recv.at[g])
                for h in range(g * group_heads, (g + 1) * group_heads):
                    piece = pl.ds(h * width, width)
                    state = above[piece, :].astype(F32) + above_factor[h : h + 1, 0:1] * ahead[piece, :].astype(F32)
                    right[piece, :] = state.astype(BF16)
                    right_send[piece, :] = (local_state[piece, :] + factor[h : h + 1, :] * state).astype(BF16)

                @pl.when(span > 0)
                def _():
                    hand_on(g)

        @pl.when(leads & (span < last_span) & (span > 1))
        def _():
            each_group(lambda g: right_copies[g].start())

        def res_copy(j):
            return pltpu.make_async_remote_copy(
                src_ref=result.at[pl.ds(j * rows, rows), :], dst_ref=res_ref.at[0, :, pl.ds(base, SPAN)],
                send_sem=res_send.at[j], recv_sem=res_recv.at[span],
                device_id=(section - 1, device_of(j)), device_id_type=MESH,
            )

        @each_group
        def _(g):
            part = pl.ds(g * group_rows, group_rows)

            @pl.when(follows)
            def _():
                landed(right.at[part, :], right_recv.at[g])

            carried = dot_nt(right[part, :], write[g])
            for j in range(g * group_devs, (g + 1) * group_devs):
                for i in range(heads_dev):
                    head = j * heads_dev + i
                    piece = pl.ds(head * width, width)
                    first = (head - g * group_heads) * width
                    reach = end_match * total[head : head + 1, :]
                    result[piece, :] = (
                        shrink[head : head + 1, :] * (inner[piece, :] + reach * carried[first : first + width, :])
                        + gains[j, heads_dev + i : heads_dev + i + 1, 0:1] * grad[piece, :].astype(F32)
                    ).astype(BF16)
                res_copy(j).start()

        for there, grad_copy, gain_copy in sends:
            @pl.when(there)
            def _():
                grad_copy.wait_send()
                gain_copy.wait_send()

        @on_core
        def _(c):
            for copy in pair_copies(c):
                copy.wait_send()

        @pl.when(follows & (span > 0))
        def _():
            factor_copy.wait_send()

        @each_group
        def _(g):
            @pl.when(leads & (span > 0))
            def _():
                right_copies[g].wait_send()

            @pl.when(leads & (span > 1))
            def _():
                ahead_copies[g].wait_send()

            @pl.when(follows & (span > 0))
            def _():
                above_copies[g].wait_send()

            for j in range(g * group_devs, (g + 1) * group_devs):
                res_copy(j).wait_send()

    @pl.when(section < last_section)
    def _():
        for z in range(spans):
            landed(res_ref.at[0, :, pl.ds(z * SPAN, SPAN)], res_recv.at[z])

    @pl.when(section == last_section)
    def _():
        zero_copy.wait()


def solution(mesh):
    sections, devs = mesh.shape["section"], mesh.shape["seq"]
    placed = (
        P("section", "seq", None),
        P("section", None, "seq"),
        P("section", "seq"),
        P("section", "seq"),
        P("section", None, "seq", None),
        P("section", None, "seq", None),
        P("section", None),
    )

    def local(grad_out, step_sizes, decay_rate, skip_gain, state_in, state_out, segment_ids):
        rows, seqlen = grad_out.shape[1:]
        heads_dev = decay_rate.shape[1]
        groups, _, state = state_in.shape[1:]
        half = devs // 2
        core_groups = group_counts(groups)[1]
        slots = core_groups * (devs // groups)
        all_rows = slots * rows
        core_heads = slots * heads_dev
        gain_rows = -(-2 * heads_dev // 8) * 8
        dma = pltpu.SemaphoreType.DMA
        anywhere = pl.BlockSpec(memory_space=pl.ANY)
        return pl.pallas_call(
            functools.partial(kernel, sections, devs),
            out_shape=pltpu.VMEM(grad_out.shape, BF16),
            in_specs=[anywhere] * 7,
            out_specs=anywhere,
            scratch_shapes=[
                pltpu.SMEM(decay_rate.shape, F32),
                pltpu.SMEM(skip_gain.shape, F32),
                pltpu.VMEM(segment_ids.shape, jnp.int32),
                pltpu.VMEM((gain_rows, LANES), F32),
                pltpu.VMEM((slots, gain_rows, LANES), F32),
                pltpu.VMEM((core_heads, LANES), F32),
                pltpu.VMEM((step_sizes.shape[1], SPAN), F32),
                pltpu.VMEM((core_heads, SPAN), F32),
                pltpu.VMEM((core_groups, SPAN, state), BF16),
                pltpu.VMEM((core_groups, SPAN, state), BF16),
                pltpu.VMEM((all_rows, SPAN), BF16),
                pltpu.VMEM((all_rows, SPAN), BF16),
                pltpu.VMEM((all_rows, SPAN), BF16),
                pltpu.VMEM((all_rows, SPAN), F32),
                pltpu.VMEM((all_rows, state), F32),
                pltpu.VMEM((all_rows, state), BF16),
                pltpu.VMEM((all_rows, state), BF16),
                pltpu.VMEM((all_rows, state), BF16),
                pltpu.VMEM((all_rows, state), BF16),
                pltpu.VMEM((core_heads, LANES), F32),
                pltpu.VMEM((core_heads, LANES), F32),
                pltpu.VMEM((all_rows, SPAN), BF16),
                pltpu.VMEM((rows, seqlen), BF16),
                dma((half,)), dma((slots,)), dma((half,)), dma((slots,)),
                dma((3,)), dma((3,)), dma((3,)),
                dma((core_groups,)), dma((core_groups,)), dma((core_groups,)),
                dma((core_groups,)), dma((core_groups,)), dma((core_groups,)), dma((2,)),
                dma((slots,)), dma((half,)), dma, dma((3,)),
            ],
            compiler_params=pltpu.CompilerParams(
                collective_id=0, has_side_effects=True, vmem_limit_bytes=64 * MIB - MIB * 3 // 4 - 2 * rows * seqlen
            ),
        )(
            grad_out, step_sizes, decay_rate, skip_gain,
            state_in, state_out, segment_ids,
        )

    return jax.shard_map(
        local, mesh=mesh, in_specs=placed, out_specs=P("section", "seq", None), check_vma=False
    )
```
